32 devices in a mesh: dp: 4 (over y, core), expert: 8 (over z, x).
Axes of the slice: x: 2, y: 2, z: 4, core: 2. Of those that a mesh axis runs over, the one named last changes fastest.
Arguments:
- tokens: bfloat16 [8192, 2048], P(('dp', 'expert')), parts along dimension 0, may hold values from -6 to 6
- target: int32 [8192, 8], P(('dp', 'expert')), parts along dimension 0, may hold values from 0 to 23, as said below
- router_weight: float32 [8192, 8], P(('dp', 'expert')), parts along dimension 0, may hold values from 0.1 to 1
- replica_pick: int32 [32], P(('dp', 'expert')), parts along dimension 0, may hold values from 0 to 1
- w_gate: bfloat16 [16, 2048, 768], P('expert'), may hold values from -0.125 to 0.125
- w_up: bfloat16 [16, 2048, 768], P('expert'), may hold values from -0.125 to 0.125
- w_down: bfloat16 [16, 768, 2048], P('expert'), may hold values from -0.21875 to 0.21875
Outputs:
- mixed: bfloat16 [8192, 2048], P(('dp', 'expert')), parts along dimension 0
The draws below stay inside these ranges and needn't reach their ends.
There are 4 independent parts, one for each index of `dp`. The reference program is written for one: setup_inputs(seed, part) draws one part's arguments, and reference() takes and returns one part's arrays. A program takes and returns all parts, laid end to end along the dimension named above; an argument that names none is the same for every part. Nothing has to cross between parts.
Inputs may be any that keep to these rules, and one draw needn't show every extreme that they name: `target`: within each aligned block of 256 rows (one device's tokens) no slot is named more than 128 times, and at least one slot, the same one in every block, is named exactly 128 times in every block (other slots may also reach 128); the 8 slots of a row name 8 different experts.
All inputs are finite; a program needn't handle non-finite values.
Results may differ from the reference program's by a relative error of at most 0.008.
Values may be sent and summed in bfloat16 or wider, within the bound.
No kernel may reach another device: no remote copies, remote signals or barrier semaphores. Data moves between devices by JAX's collectives and lax.ppermute only.
A program may use at most 192 MiB of HBM per device.

```python
import math
import jax
import jax.numpy as jnp
from jax import lax

D = 2048
FF = 768
TOP = 8
EXP_DEV = 2
TOK_DEV = 256
EXPERTS = 16
TOKENS = 2048
CAP = 128
N_EXPERT = 8


def lent_choices(key):
    return jax.random.randint(jax.random.fold_in(key, 11), (N_EXPERT,), 0, EXP_DEV).astype(jnp.int32)


def draw_replica_pick(key, part):
    return lent_choices(key)


def draw_target(key, part):
    pick = lent_choices(key)
    slots = EXP_DEV + 1
    virtual = N_EXPERT * slots
    labels = jnp.arange(virtual, dtype=jnp.int32)
    hosts = labels // slots
    local = labels % slots
    left = (hosts - 1) % N_EXPERT
    order_key = jnp.where(local < EXP_DEV, 2 * (hosts * EXP_DEV + local), 2 * (left * EXP_DEV + pick[left]) + 1)
    order = jnp.argsort(order_key).astype(jnp.int32)
    hot_slot = jax.random.randint(jax.random.fold_in(key, 12), (), 0, virtual)
    many = virtual // 4
    total = TOK_DEV * TOP
    rest = total - many * CAP
    cold = virtual - many

    def block(index):
        block_key = jax.random.fold_in(jax.random.fold_in(key, 13), index)
        scores = jax.random.permutation(jax.random.fold_in(block_key, 1), virtual).astype(jnp.int32)
        scores = jnp.where(labels == hot_slot, -1, scores)
        ranking = jnp.argsort(jnp.argsort(scores)).astype(jnp.int32)
        extra = (ranking - many < rest % cold).astype(jnp.int32)
        load = jnp.where(ranking < many, CAP, rest // cold + extra)
        ends = jnp.cumsum(load[order])
        position = jnp.arange(total, dtype=jnp.int32)
        which = jnp.sum((position[:, None] >= ends[None, :]).astype(jnp.int32), axis=1)
        listed = order[which].reshape(TOP, TOK_DEV)
        shuffle = jax.random.permutation(jax.random.fold_in(block_key, 2), TOK_DEV)
        return listed[:, shuffle].T
    blocks = jax.vmap(block)(jnp.arange(N_EXPERT, dtype=jnp.int32))
    return blocks.reshape(TOKENS, TOP).astype(jnp.int32)


def levels(own_key, extent, cuts, smallest, top_value):
    loudness = 1.0
    for dim, shards_of in cuts:
        draws = jax.random.uniform(jax.random.fold_in(jax.random.fold_in(own_key, 6), dim), (shards_of,), jnp.float32, smallest / len(cuts), top_value / len(cuts))
        loudness = loudness * jnp.repeat(jnp.exp(draws), extent[dim] // shards_of).reshape((-1,) + (1,) * (len(extent) - 1 - dim))
    return loudness


def centred(stream_key, extent, deviation, reach, cuts=(), kind=jnp.bfloat16):
    result = deviation * jax.random.normal(stream_key, extent, jnp.float32)
    if cuts:
        result = result * levels(stream_key, extent, cuts, -0.22, 0.18)
    return jnp.clip(result, -reach, reach).astype(kind)


def setup_inputs(seed: int = 0, part: int = 0) -> dict:
    key_list = jax.random.split(jax.random.key(seed), 8)
    part_keys = jax.random.split(jax.random.fold_in(key_list[7], part), 8)
    tokens = centred(part_keys[0], (TOKENS, D), 1.0, 6.0, ((0, 8),))
    target = draw_target(jax.random.fold_in(jax.random.fold_in(key_list[7], part), 71), part)
    router_weight = jnp.clip(jnp.exp(math.log(1.0) - 2.3025851 * jax.random.uniform(part_keys[2], (TOKENS, TOP), jnp.float32) ** levels(part_keys[2], (TOKENS, TOP), ((0, 8),), -0.2, 0.2)), 0.1, 1.0)
    replica_pick = draw_replica_pick(jax.random.fold_in(jax.random.fold_in(key_list[7], part), 71), part)
    w_gate = centred(key_list[4], (EXPERTS, D, FF), D ** -0.5, 0.125, ((0, 8),))
    w_up = centred(key_list[5], (EXPERTS, D, FF), D ** -0.5, 0.125, ((0, 8),))
    w_down = centred(key_list[6], (EXPERTS, FF, D), FF ** -0.5, 0.21875, ((0, 8),))
    return dict(tokens=tokens, target=target, router_weight=router_weight, replica_pick=replica_pick, w_gate=w_gate, w_up=w_up, w_down=w_down)


def reference(tokens, target, router_weight, replica_pick, w_gate, w_up, w_down):
    slots = EXP_DEV + 1
    host = target // slots
    local = target % slots
    left = (host - 1) % N_EXPERT
    expert_id = jnp.where(local < EXP_DEV, host * EXP_DEV + local, left * EXP_DEV + replica_pick[left]).astype(jnp.int32)
    share = router_weight / jnp.sum(router_weight, axis=1, keepdims=True)

    def step(total, item):
        weight_gate, weight_up, weight_down, which = item
        coeff = jnp.sum(jnp.where(expert_id == which, share, jnp.zeros_like(share)), axis=1)
        gate = jnp.dot(tokens, weight_gate, preferred_element_type=jnp.float32)
        upper = jnp.dot(tokens, weight_up, preferred_element_type=jnp.float32)
        hidden = (jax.nn.silu(gate) * upper).astype(jnp.bfloat16)
        output = jnp.dot(hidden, weight_down, preferred_element_type=jnp.float32).astype(jnp.bfloat16)
        return total + coeff[:, None] * output.astype(total.dtype), None

    start = jnp.zeros((TOKENS, D), jnp.float32)
    total, unused = lax.scan(step, start, (w_gate, w_up, w_down, jnp.arange(EXPERTS, dtype=jnp.int32)))
    return total.astype(jnp.bfloat16)
```

```python
import functools

import jax
import jax.numpy as jnp
from jax import lax
from jax.experimental import pallas as pl
from jax.experimental.pallas import tpu as pltpu
from jax.sharding import PartitionSpec as P


def ring_order(groups):
    columns = 1 << ((groups.bit_length() - 1) // 2)
    rows = groups // columns
    walk = [z * columns for z in range(rows)]
    for turn, z in enumerate(reversed(range(rows))):
        row = [z * columns + x for x in range(1, columns)]
        walk += row if turn % 2 == 0 else row[::-1]
    return walk


def expert_kernel(tiles, count, *refs):
    chunks = refs[:count]
    coeff_ref, gate_ref, up_ref, down_ref = refs[count:count + 4]
    outs = refs[count + 4:2 * count + 4]
    rows_ref, total_ref = refs[2 * count + 4:]
    step = pl.program_id(0)
    height = chunks[0].shape[0]

    @pl.when(step == 0)
    def _():
        for i in range(count):
            rows_ref[i * height:(i + 1) * height, :] = chunks[i][...]

    x = rows_ref[...]
    gate = jnp.dot(x, gate_ref[0], preferred_element_type=jnp.float32)
    upper = jnp.dot(x, up_ref[0], preferred_element_type=jnp.float32)
    coeff = coeff_ref[...]
    lane = lax.broadcasted_iota(jnp.int32, coeff.shape, 1)
    share = jnp.sum(jnp.where(lane == step // tiles, coeff, 0.0), axis=1, keepdims=True)
    hidden = (gate / (1.0 + jnp.exp(-gate)) * upper * share).astype(jnp.bfloat16)
    part = jnp.dot(hidden, down_ref[0], preferred_element_type=jnp.float32)

    @pl.when(step == 0)
    def _():
        total_ref[...] = part

    @pl.when(step > 0)
    def _():
        total_ref[...] += part

    @pl.when(step == pl.num_programs(0) - 1)
    def _():
        for i in range(count):
            outs[i][...] = total_ref[i * height:(i + 1) * height, :].astype(outs[i].dtype)


def experts(chunks, coeffs, w_gate, w_up, w_down):
    count = len(chunks)
    height, width = chunks[0].shape
    owned, unused, units = w_gate.shape
    tile = 256 if units % 256 == 0 else units
    tiles = units // tile
    rows = count * height
    coeff = jnp.concatenate(coeffs, axis=0) if count > 1 else coeffs[0]
    whole = pl.BlockSpec((height, width), lambda j: (0, 0))
    flops = 6 * rows * width * units * owned
    moved = 2 * 3 * owned * width * units + 4 * rows * width
    return pl.pallas_call(
        functools.partial(expert_kernel, tiles, count),
        grid=(owned * tiles,),
        in_specs=[whole] * count + [
            pl.BlockSpec((rows, coeff.shape[1]), lambda j: (0, 0)),
            pl.BlockSpec((1, width, tile), lambda j: (j // tiles, 0, j % tiles)),
            pl.BlockSpec((1, width, tile), lambda j: (j // tiles, 0, j % tiles)),
            pl.BlockSpec((1, tile, width), lambda j: (j // tiles, j % tiles, 0)),
        ],
        out_specs=[whole] * count,
        out_shape=[jax.ShapeDtypeStruct((height, width), jnp.bfloat16)] * count,
        scratch_shapes=[pltpu.VMEM((rows, width), jnp.bfloat16), pltpu.VMEM((rows, width), jnp.float32)],
        compiler_params=pltpu.CompilerParams(vmem_limit_bytes=48 * 1024 * 1024),
        cost_estimate=pl.CostEstimate(flops=flops, bytes_accessed=moved, transcendentals=rows * units * owned),
    )(*chunks, coeff, w_gate, w_up, w_down)


def body(tokens, target, router_weight, replica_pick, w_gate, w_up, w_down):
    height, width = tokens.shape
    owned = w_gate.shape[0]
    slots = owned + 1
    groups = lax.axis_size("expert")
    me = lax.axis_index("expert")
    walk = ring_order(groups)
    place = [walk.index(i) for i in range(groups)]
    ahead = [(walk[i], walk[(i + 1) % groups]) for i in range(groups)]
    back = [(b, a) for a, b in ahead]
    position = jnp.asarray(place, jnp.int32)[me]
    order = jnp.asarray(walk, jnp.int32)

    share = router_weight / jnp.sum(router_weight, axis=1, keepdims=True)
    label = jnp.arange(groups * slots, dtype=jnp.int32)
    table = jnp.sum(jnp.where(target.T[None, :, :] == label[:, None, None], share.T[None, :, :], 0.0), axis=1)
    tables = lax.all_gather(table, "expert", axis=0, tiled=False)
    mine = lax.dynamic_slice_in_dim(tables, me * slots, owned, axis=1)
    lent = lax.dynamic_index_in_dim(tables, lax.rem(me + 1, groups) * slots + owned, 1, keepdims=True)
    which = lax.broadcasted_iota(jnp.int32, (1, owned, 1), 1)
    coeffs = jnp.swapaxes(mine + jnp.where(which == replica_pick[0], lent, 0.0), 1, 2)

    def coeff(offset):
        owner = order[lax.rem(position + offset + groups, groups)]
        return lax.dynamic_index_in_dim(coeffs, owner, 0, keepdims=False)

    run = functools.partial(experts, w_gate=w_gate, w_up=w_up, w_down=w_down)
    far = groups // 2
    half = height // 2
    from_left, from_right = tokens, tokens
    left_parts, right_parts = {}, {}
    for s in range(1, far):
        from_left = lax.ppermute(from_left, "expert", ahead)
        from_right = lax.ppermute(from_right, "expert", back)
        if s == 1:
            own_part, = run([tokens], [coeff(0)])
        left_parts[s], right_parts[s] = run([from_left, from_right], [coeff(-s), coeff(s)])
    top_half = lax.ppermute(from_left[:half], "expert", ahead)
    low_half = lax.ppermute(from_right[half:], "expert", back)
    far_coeff = coeff(far)
    top_part, low_part = run([top_half, low_half], [far_coeff[:half], far_coeff[half:]])

    def add(a, b):
        return (a.astype(jnp.float32) + b.astype(jnp.float32)).astype(jnp.bfloat16)

    to_left = lax.ppermute(top_part, "expert", back)
    to_right = lax.ppermute(low_part, "expert", ahead)
    for s in range(far - 1, 0, -1):
        left, right = left_parts[s], right_parts[s]
        if s == far - 1:
            left = jnp.concatenate([add(left[:half], to_left), left[half:]], axis=0)
            right = jnp.concatenate([right[:half], add(right[half:], to_right)], axis=0)
        else:
            left, right = add(left, to_left), add(right, to_right)
        to_left = lax.ppermute(left, "expert", back)
        to_right = lax.ppermute(right, "expert", ahead)
    total = own_part.astype(jnp.float32) + to_left.astype(jnp.float32) + to_right.astype(jnp.float32)
    return total.astype(jnp.bfloat16)


def solution(mesh):
    in_specs = (
        P(("dp", "expert"), None),
        P(("dp", "expert"), None),
        P(("dp", "expert"), None),
        P(("dp", "expert")),
        P("expert", None, None),
        P("expert", None, None),
        P("expert", None, None),
    )
    out_specs = P(("dp", "expert"), None)
    return jax.shard_map(body, mesh=mesh, in_specs=in_specs, out_specs=out_specs, check_vma=False)
```

```python
import functools

import jax
import jax.numpy as jnp
from jax import lax
from jax.experimental import pallas as pl
from jax.experimental.pallas import tpu as pltpu
from jax.sharding import PartitionSpec as P

VMEM_LIMIT = 48 * 1024 * 1024


def ring_order(groups):
    columns = 1 << ((groups.bit_length() - 1) // 2)
    rows = groups // columns
    walk = [z * columns for z in range(rows)]
    for turn, z in enumerate(reversed(range(rows))):
        row = [z * columns + x for x in range(1, columns)]
        walk += row if turn % 2 == 0 else row[::-1]
    return walk


def table_rows(slots, height, width):
    one = -(-slots * height // width)
    return one, -(-2 * one // 8) * 8


def pack_kernel(slots, tokens_ref, target_ref, weight_ref, out_ref):
    half, width = out_ref.shape[0], out_ref.shape[1]
    height = tokens_ref.shape[0]
    half = height // 2
    one, extra = table_rows(slots, height, width)
    per_row = width // height
    out_ref[:half, :] = tokens_ref[:half, :]
    weight = weight_ref[...]
    share = weight / jnp.sum(weight, axis=0, keepdims=True)
    target = target_ref[...]
    row = lax.broadcasted_iota(jnp.int32, (extra, height), 0)
    for lane in range(per_row):
        block = jnp.zeros((extra, height), jnp.float32)
        for r in range(one):
            slot = r * per_row + lane
            if slot < slots:
                value = jnp.sum(jnp.where(target == slot, share, 0.0), axis=0, keepdims=True)
                high = value.astype(jnp.bfloat16).astype(jnp.float32)
                block = jnp.where(row == r, high, block)
                block = jnp.where(row == one + r, value - high, block)
        out_ref[half:, lane * height:(lane + 1) * height] = block.astype(jnp.bfloat16)


def pack(tokens, target, router_weight, slots):
    height, width = tokens.shape
    extra = table_rows(slots, height, width)[1]
    return pl.pallas_call(
        functools.partial(pack_kernel, slots),
        out_shape=jax.ShapeDtypeStruct((height // 2 + extra, width), jnp.bfloat16),
        compiler_params=pltpu.CompilerParams(vmem_limit_bytes=VMEM_LIMIT),
    )(tokens, target.T, router_weight.T)


def expert_kernel(plan, place_ref, *refs):
    tiles, steps, parts, tables, slots, height = plan
    count = len(parts)
    chunks = refs[:count]
    table_refs = refs[count:count + tables]
    gate_ref, up_ref, down_ref = refs[count + tables:count + tables + 3]
    outs = refs[count + tables + 3:2 * count + tables + 3]
    rows_ref, hidden_ref, share_ref = refs[2 * count + tables + 3:]
    step = pl.program_id(0)
    half = height // 2
    width = rows_ref.shape[1]
    tile = gate_ref.shape[2]
    owned = hidden_ref.shape[1] // (tile * tiles)

    @pl.when(step == 0)
    def _():
        one, extra = table_rows(slots, height, width)
        per_row = width // height
        me, after, pick = place_ref[0], place_ref[1], place_ref[2]

        def column(ref, slot):
            lane = pl.multiple_of(lax.rem(slot, per_row) * height, height)
            block = ref[half:half + extra, pl.ds(lane, height)].astype(jnp.float32)
            row = lax.broadcasted_iota(jnp.int32, block.shape, 0)
            line = lax.div(slot, per_row)
            return jnp.sum(jnp.where((row == line) | (row == one + line), block, 0.0), axis=0, keepdims=True)

        columns = []
        for ref in table_refs:
            lent = column(ref, after * (owned + 1) + owned)
            lines = [column(ref, me * (owned + 1) + e) + jnp.where(pick == e, lent, 0.0) for e in range(owned)]
            row = lax.broadcasted_iota(jnp.int32, (128, height), 0)
            block = jnp.zeros((128, height), jnp.float32)
            for e in range(owned):
                block = jnp.where(row == e, lines[e], block)
            columns.append(block.T)
        for i, (which, first) in enumerate(parts):
            rows_ref[i * half:(i + 1) * half, :] = chunks[i][:half, :]
            share_ref[i * half:(i + 1) * half, :] = columns[which][first:first + half, :]

    @pl.when(step < steps)
    def _():
        x = rows_ref[...]
        gate = jnp.dot(x, gate_ref[0], preferred_element_type=jnp.float32)
        upper = jnp.dot(x, up_ref[0], preferred_element_type=jnp.float32)
        share = share_ref[...]
        lane = lax.broadcasted_iota(jnp.int32, share.shape, 1)
        share = jnp.sum(jnp.where(lane == step // tiles, share, 0.0), axis=1, keepdims=True)
        hidden = gate / (1.0 + jnp.exp(-gate)) * upper * share
        hidden_ref[:, pl.ds(pl.multiple_of(step * tile, tile), tile)] = hidden.astype(jnp.bfloat16)

    @pl.when(step >= steps)
    def _():
        part = jnp.dot(hidden_ref[...], down_ref[...], preferred_element_type=jnp.float32)
        for i in range(count):
            outs[i][...] = part[i * half:(i + 1) * half].astype(jnp.bfloat16)


def experts(place, chunks, tables, parts, slots, height, w_gate, w_up, w_down):
    count, half = len(chunks), height // 2
    owned, width, units = w_gate.shape
    tile = units
    tiles = units // tile
    steps = owned * tiles
    wide = width // 2
    rows = count * half
    last = steps - 1

    def whole(a):
        return pl.BlockSpec(a.shape, lambda j, place: (0, 0))

    def projection(j, place):
        at = jnp.minimum(j, last)
        return at // tiles, 0, at % tiles

    def across(j, place):
        return 0, jnp.maximum(j - steps, 0)

    flops = 6 * rows * width * units * owned
    moved = 2 * 3 * owned * width * units + 4 * rows * width
    return pl.pallas_call(
        functools.partial(expert_kernel, (tiles, steps, parts, len(tables), slots, height)),
        grid_spec=pltpu.PrefetchScalarGridSpec(
            num_scalar_prefetch=1,
            grid=(steps + width // wide,),
            in_specs=[whole(a) for a in chunks] + [whole(a) for a in tables] + [
                pl.BlockSpec((1, width, tile), projection),
                pl.BlockSpec((1, width, tile), projection),
                pl.BlockSpec((owned * units, wide), across),
            ],
            out_specs=[pl.BlockSpec((half, wide), across)] * count,
            scratch_shapes=[
                pltpu.VMEM((rows, width), jnp.bfloat16),
                pltpu.VMEM((rows, owned * units), jnp.bfloat16),
                pltpu.VMEM((rows, 128), jnp.float32),
            ],
        ),
        out_shape=[jax.ShapeDtypeStruct((half, width), jnp.bfloat16)] * count,
        compiler_params=pltpu.CompilerParams(vmem_limit_bytes=VMEM_LIMIT),
        cost_estimate=pl.CostEstimate(flops=flops, bytes_accessed=moved, transcendentals=rows * units * owned),
    )(place, *chunks, *tables, w_gate, w_up, w_down.reshape(owned * units, width))


def add(a, b):
    return (a.astype(jnp.float32) + b.astype(jnp.float32)).astype(jnp.bfloat16)


def body(tokens, target, router_weight, replica_pick, w_gate, w_up, w_down):
    height, width = tokens.shape
    half = height // 2
    groups = lax.axis_size("expert")
    slots = groups * (w_gate.shape[0] + 1)
    walk = ring_order(groups)
    ahead = [(walk[i], walk[(i + 1) % groups]) for i in range(groups)]
    back = [(b, a) for a, b in ahead]
    me = lax.axis_index("expert").astype(jnp.int32)
    after = jnp.where(me == groups - 1, 0, me + 1)
    place = jnp.stack([me, after, replica_pick[0]])
    run = functools.partial(experts, place, slots=slots, height=height, w_gate=w_gate, w_up=w_up, w_down=w_down)

    first_a = pack(tokens, target, router_weight, slots)
    first_b = tokens[half:]
    far = groups // 2
    a_left, b_left, a_right, b_right = first_a, first_b, first_a, first_b
    parts = {}
    for s in range(1, far):
        a_left = lax.ppermute(a_left, "expert", ahead)
        b_right = lax.ppermute(b_right, "expert", back)
        a_right = lax.ppermute(a_right, "expert", back)
        b_left = lax.ppermute(b_left, "expert", ahead)
        if s == 1:
            own = run([first_a, first_b], [first_a], ((0, 0), (0, half)))
        parts[s] = run([a_left, b_left, a_right, b_right], [a_left, a_right], ((0, 0), (0, half), (1, 0), (1, half)))
    a_left = lax.ppermute(a_left, "expert", ahead)
    table_right = a_right
    b_right = lax.ppermute(b_right, "expert", back)
    far_a, far_b = run([a_left, b_right], [a_left], ((0, 0), (0, half)))

    a_to_left = lax.ppermute(far_a, "expert", back)
    b_to_right = lax.ppermute(far_b, "expert", ahead)
    a_to_right = b_to_left = None
    for s in range(far - 1, 0, -1):
        pa_left, pb_left, pa_right, pb_right = parts[s]
        a_to_left = lax.ppermute(add(pa_left, a_to_left), "expert", back)
        b_to_right = lax.ppermute(add(pb_right, b_to_right), "expert", ahead)
        a_to_right = lax.ppermute(pa_right if a_to_right is None else add(pa_right, a_to_right), "expert", ahead)
        b_to_left = lax.ppermute(pb_left if b_to_left is None else add(pb_left, b_to_left), "expert", back)

    def final(own_part, x, y):
        return (own_part.astype(jnp.float32) + x.astype(jnp.float32) + y.astype(jnp.float32)).astype(jnp.bfloat16)

    return jnp.concatenate([final(own[0], a_to_left, a_to_right), final(own[1], b_to_left, b_to_right)], axis=0)


def solution(mesh):
    in_specs = (
        P(("dp", "expert"), None),
        P(("dp", "expert"), None),
        P(("dp", "expert"), None),
        P(("dp", "expert")),
        P("expert", None, None),
        P("expert", None, None),
        P("expert", None, None),
    )
    out_specs = P(("dp", "expert"), None)
    return jax.shard_map(body, mesh=mesh, in_specs=in_specs, out_specs=out_specs, check_vma=False)
```

```python
import functools

import jax
import jax.numpy as jnp
from jax import lax
from jax.experimental import pallas as pl
from jax.experimental.pallas import tpu as pltpu
from jax.sharding import PartitionSpec as P

VMEM_LIMIT = 16 * 1024 * 1024


def ring_order(groups):
    columns = 1 << ((groups.bit_length() - 1) // 2)
    rows = groups // columns
    walk = [z * columns for z in range(rows)]
    for turn, z in enumerate(reversed(range(rows))):
        row = [z * columns + x for x in range(1, columns)]
        walk += row if turn % 2 == 0 else row[::-1]
    return walk


def table_rows(slots, height, width):
    one = -(-slots * height // width)
    return one, -(-2 * one // 8) * 8


def pack_kernel(slots, tokens_ref, target_ref, weight_ref, out_ref):
    half, width = out_ref.shape[0], out_ref.shape[1]
    height = tokens_ref.shape[0]
    half = height // 2
    one, extra = table_rows(slots, height, width)
    per_row = width // height
    out_ref[:half, :] = tokens_ref[:half, :]
    weight = weight_ref[...]
    share = weight / jnp.sum(weight, axis=0, keepdims=True)
    target = target_ref[...]
    row = lax.broadcasted_iota(jnp.int32, (extra, height), 0)
    for lane in range(per_row):
        block = jnp.zeros((extra, height), jnp.float32)
        for r in range(one):
            slot = r * per_row + lane
            if slot < slots:
                value = jnp.sum(jnp.where(target == slot, share, 0.0), axis=0, keepdims=True)
                high = value.astype(jnp.bfloat16).astype(jnp.float32)
                block = jnp.where(row == r, high, block)
                block = jnp.where(row == one + r, value - high, block)
        out_ref[half:, lane * height:(lane + 1) * height] = block.astype(jnp.bfloat16)


def pack(tokens, target, router_weight, slots):
    height, width = tokens.shape
    extra = table_rows(slots, height, width)[1]
    return pl.pallas_call(
        functools.partial(pack_kernel, slots),
        out_shape=jax.ShapeDtypeStruct((height // 2 + extra, width), jnp.bfloat16),
        compiler_params=pltpu.CompilerParams(vmem_limit_bytes=VMEM_LIMIT),
    )(tokens, target.T, router_weight.T)


def expert_kernel(first, slots, height, place_ref, chunk_ref, table_ref, gate_ref, up_ref, down_ref, out_ref, hidden_ref):
    half = height // 2
    owned, width, units = gate_ref.shape
    one, extra = table_rows(slots, height, width)
    per_row = width // height
    me, after, pick = place_ref[0], place_ref[1], place_ref[2]

    def column(slot):
        lane = pl.multiple_of(lax.rem(slot, per_row) * height + first, half)
        block = table_ref[half:half + extra, pl.ds(lane, half)].astype(jnp.float32)
        row = lax.broadcasted_iota(jnp.int32, block.shape, 0)
        line = lax.div(slot, per_row)
        return jnp.sum(jnp.where((row == line) | (row == one + line), block, 0.0), axis=0, keepdims=True)

    lent = column(after * (owned + 1) + owned)
    row = lax.broadcasted_iota(jnp.int32, (128, half), 0)
    shares = jnp.zeros((128, half), jnp.float32)
    for e in range(owned):
        line = column(me * (owned + 1) + e) + jnp.where(pick == e, lent, 0.0)
        shares = jnp.where(row == e, line, shares)
    shares = shares.T

    x = chunk_ref[:half, :]
    for e in range(owned):
        gate = jnp.dot(x, gate_ref[e], preferred_element_type=jnp.float32)
        upper = jnp.dot(x, up_ref[e], preferred_element_type=jnp.float32)
        hidden = gate / (1.0 + jnp.exp(-gate)) * upper * shares[:, e:e + 1]
        hidden_ref[:, e * units:(e + 1) * units] = hidden.astype(jnp.bfloat16)
    out_ref[...] = jnp.dot(hidden_ref[...], down_ref[...], preferred_element_type=jnp.float32).astype(jnp.bfloat16)


def experts(place, weights, slots, height, chunk, table, first):
    half = height // 2
    w_gate, w_up, w_down = weights
    owned, width, units = w_gate.shape
    flops = 6 * half * width * units * owned
    vmem = pl.BlockSpec(memory_space=pltpu.VMEM)
    return pl.pallas_call(
        functools.partial(expert_kernel, first, slots, height),
        in_specs=[pl.BlockSpec(memory_space=pltpu.SMEM)] + [vmem] * 5,
        out_specs=vmem,
        out_shape=jax.ShapeDtypeStruct((half, width), jnp.bfloat16),
        scratch_shapes=[pltpu.VMEM((half, owned * units), jnp.bfloat16)],
        compiler_params=pltpu.CompilerParams(vmem_limit_bytes=VMEM_LIMIT),
        cost_estimate=pl.CostEstimate(flops=flops, bytes_accessed=8 * half * width, transcendentals=half * units * owned),
    )(place, chunk, table, w_gate, w_up, w_down)


def add(a, b):
    return (a.astype(jnp.float32) + b.astype(jnp.float32)).astype(jnp.bfloat16)


def body(tokens, target, router_weight, replica_pick, w_gate, w_up, w_down):
    height, width = tokens.shape
    half = height // 2
    groups = lax.axis_size("expert")
    slots = groups * (w_gate.shape[0] + 1)
    walk = ring_order(groups)
    ahead = [(walk[i], walk[(i + 1) % groups]) for i in range(groups)]
    back = [(b, a) for a, b in ahead]
    me = lax.axis_index("expert").astype(jnp.int32)
    after = jnp.where(me == groups - 1, 0, me + 1)
    place = jnp.stack([me, after, replica_pick[0]])
    weights = w_gate, w_up, w_down.reshape(-1, width)
    run = functools.partial(experts, place, weights, slots, height)

    first_a = pack(tokens, target, router_weight, slots)
    first_b = tokens[half:]
    far = groups // 2
    a_left, b_left, a_right, b_right = first_a, first_b, first_a, first_b
    parts = {}
    own = run(first_a, first_a, 0), run(first_b, first_a, half)
    for s in range(1, far):
        a_left = lax.ppermute(a_left, "expert", ahead)
        b_right = lax.ppermute(b_right, "expert", back)
        a_right = lax.ppermute(a_right, "expert", back)
        b_left = lax.ppermute(b_left, "expert", ahead)
        parts[s] = run(a_left, a_left, 0), run(b_left, a_left, half), run(a_right, a_right, 0), run(b_right, a_right, half)
    a_left = lax.ppermute(a_left, "expert", ahead)
    b_right = lax.ppermute(b_right, "expert", back)
    far_a, far_b = run(a_left, a_left, 0), run(b_right, a_left, half)

    a_to_left = lax.ppermute(far_a, "expert", back)
    b_to_right = lax.ppermute(far_b, "expert", ahead)
    a_to_right = b_to_left = None
    for s in range(far - 1, 0, -1):
        pa_left, pb_left, pa_right, pb_right = parts[s]
        a_to_left = lax.ppermute(add(pa_left, a_to_left), "expert", back)
        b_to_right = lax.ppermute(add(pb_right, b_to_right), "expert", ahead)
        a_to_right = lax.ppermute(pa_right if a_to_right is None else add(pa_right, a_to_right), "expert", ahead)
        b_to_left = lax.ppermute(pb_left if b_to_left is None else add(pb_left, b_to_left), "expert", back)

    def final(own_part, x, y):
        return (own_part.astype(jnp.float32) + x.astype(jnp.float32) + y.astype(jnp.float32)).astype(jnp.bfloat16)

    return jnp.concatenate([final(own[0], a_to_left, a_to_right), final(own[1], b_to_left, b_to_right)], axis=0)


def solution(mesh):
    in_specs = (
        P(("dp", "expert"), None),
        P(("dp", "expert"), None),
        P(("dp", "expert"), None),
        P(("dp", "expert")),
        P("expert", None, None),
        P("expert", None, None),
        P("expert", None, None),
    )
    out_specs = P(("dp", "expert"), None)
    return jax.shard_map(body, mesh=mesh, in_specs=in_specs, out_specs=out_specs, check_vma=False)
```

```python
import functools

import jax
import jax.numpy as jnp
from jax import lax
from jax.experimental import pallas as pl
from jax.experimental.pallas import tpu as pltpu
from jax.sharding import PartitionSpec as P

VMEM_LIMIT = 16 * 1024 * 1024
WIDE_LIMIT = 56 * 1024 * 1024


def ring_order(groups):
    columns = 1 << ((groups.bit_length() - 1) // 2)
    rows = groups // columns
    walk = [z * columns for z in range(rows)]
    for turn, z in enumerate(reversed(range(rows))):
        row = [z * columns + x for x in range(1, columns)]
        walk += row if turn % 2 == 0 else row[::-1]
    return walk


def table_rows(slots, height, width):
    one = -(-slots * height // width)
    return one, -(-2 * one // 8) * 8


def pack_kernel(slots, tokens_ref, target_ref, weight_ref, a_ref, b_ref, target_buf, weight_buf, sems):
    height, width = tokens_ref.shape
    half = height // 2
    one, extra = table_rows(slots, height, width)
    per_row = width // height
    copies = [
        pltpu.make_async_copy(target_ref, target_buf, sems.at[0]),
        pltpu.make_async_copy(weight_ref, weight_buf, sems.at[1]),
        pltpu.make_async_copy(tokens_ref.at[pl.ds(half, half)], b_ref, sems.at[2]),
        pltpu.make_async_copy(tokens_ref.at[pl.ds(0, half)], a_ref.at[pl.ds(0, half)], sems.at[3]),
    ]
    for copy in copies:
        copy.start()
    copies[0].wait()
    copies[1].wait()
    weight = weight_buf[...]
    share = weight / jnp.sum(weight, axis=0, keepdims=True)
    target = target_buf[...]
    row = lax.broadcasted_iota(jnp.int32, (extra, height), 0)
    for lane in range(per_row):
        block = jnp.zeros((extra, height), jnp.float32)
        for r in range(one):
            slot = r * per_row + lane
            if slot < slots:
                value = jnp.sum(jnp.where(target == slot, share, 0.0), axis=0, keepdims=True)
                high = value.astype(jnp.bfloat16).astype(jnp.float32)
                block = jnp.where(row == r, high, block)
                block = jnp.where(row == one + r, value - high, block)
        a_ref[half:, lane * height:(lane + 1) * height] = block.astype(jnp.bfloat16)
    copies[2].wait()
    copies[3].wait()


def pack(tokens, target, router_weight, slots):
    height, width = tokens.shape
    half, top = height // 2, target.shape[1]
    extra = table_rows(slots, height, width)[1]
    vmem = pl.BlockSpec(memory_space=pltpu.VMEM)
    return pl.pallas_call(
        functools.partial(pack_kernel, slots),
        in_specs=[pl.BlockSpec(memory_space=pl.ANY)] * 3,
        out_specs=[vmem, vmem],
        out_shape=[
            jax.ShapeDtypeStruct((half + extra, width), jnp.bfloat16),
            jax.ShapeDtypeStruct((half, width), jnp.bfloat16),
        ],
        scratch_shapes=[
            pltpu.VMEM((top, height), jnp.int32),
            pltpu.VMEM((top, height), jnp.float32),
            pltpu.SemaphoreType.DMA((4,)),
        ],
        compiler_params=pltpu.CompilerParams(vmem_limit_bytes=WIDE_LIMIT),
        cost_estimate=pl.CostEstimate(flops=0, bytes_accessed=4 * height * width, transcendentals=0),
    )(tokens, target.T, router_weight.T)


def expert_kernel(first, slots, height, place_ref, chunk_ref, table_ref, gate_ref, up_ref, down_ref, out_ref, hidden_ref):
    half = height // 2
    owned, width, units = gate_ref.shape
    one, extra = table_rows(slots, height, width)
    per_row = width // height
    me, after, pick = place_ref[0], place_ref[1], place_ref[2]

    def column(slot):
        lane = pl.multiple_of(lax.rem(slot, per_row) * height + first, half)
        block = table_ref[half:half + extra, pl.ds(lane, half)].astype(jnp.float32)
        row = lax.broadcasted_iota(jnp.int32, block.shape, 0)
        line = lax.div(slot, per_row)
        return jnp.sum(jnp.where((row == line) | (row == one + line), block, 0.0), axis=0, keepdims=True)

    lent = column(after * (owned + 1) + owned)
    row = lax.broadcasted_iota(jnp.int32, (128, half), 0)
    shares = jnp.zeros((128, half), jnp.float32)
    for e in range(owned):
        line = column(me * (owned + 1) + e) + jnp.where(pick == e, lent, 0.0)
        shares = jnp.where(row == e, line, shares)
    shares = shares.T

    x = chunk_ref[:half, :]
    for e in range(owned):
        gate = jnp.dot(x, gate_ref[e], preferred_element_type=jnp.float32)
        upper = jnp.dot(x, up_ref[e], preferred_element_type=jnp.float32)
        hidden = gate / (1.0 + jnp.exp(-gate)) * upper * shares[:, e:e + 1]
        hidden_ref[:, e * units:(e + 1) * units] = hidden.astype(jnp.bfloat16)
    out_ref[...] = jnp.dot(hidden_ref[...], down_ref[...], preferred_element_type=jnp.float32).astype(jnp.bfloat16)


def experts(place, weights, slots, height, chunk, table, first):
    half = height // 2
    w_gate, w_up, w_down = weights
    owned, width, units = w_gate.shape
    flops = 6 * half * width * units * owned
    vmem = pl.BlockSpec(memory_space=pltpu.VMEM)
    return pl.pallas_call(
        functools.partial(expert_kernel, first, slots, height),
        in_specs=[pl.BlockSpec(memory_space=pltpu.SMEM)] + [vmem] * 5,
        out_specs=vmem,
        out_shape=jax.ShapeDtypeStruct((half, width), jnp.bfloat16),
        scratch_shapes=[pltpu.VMEM((half, owned * units), jnp.bfloat16)],
        compiler_params=pltpu.CompilerParams(vmem_limit_bytes=VMEM_LIMIT),
        cost_estimate=pl.CostEstimate(flops=flops, bytes_accessed=8 * half * width, transcendentals=half * units * owned),
    )(place, chunk, table, w_gate, w_up, w_down)


def finish_kernel(*refs):
    out_ref = refs[-1]
    half = refs[0].shape[0]
    for i in range(2):
        total = sum(ref[...].astype(jnp.float32) for ref in refs[3 * i:3 * i + 3])
        out_ref[i * half:(i + 1) * half, :] = total.astype(out_ref.dtype)


def finish(a, b):
    half, width = a[0].shape
    vmem = pl.BlockSpec(memory_space=pltpu.VMEM)
    return pl.pallas_call(
        finish_kernel,
        in_specs=[vmem] * 6,
        out_specs=vmem,
        out_shape=jax.ShapeDtypeStruct((2 * half, width), a[0].dtype),
        compiler_params=pltpu.CompilerParams(vmem_limit_bytes=VMEM_LIMIT),
    )(*a, *b)


def add(a, b):
    return (a.astype(jnp.float32) + b.astype(jnp.float32)).astype(jnp.bfloat16)


def body(tokens, target, router_weight, replica_pick, w_gate, w_up, w_down):
    height, width = tokens.shape
    half = height // 2
    groups = lax.axis_size("expert")
    slots = groups * (w_gate.shape[0] + 1)
    walk = ring_order(groups)
    ahead = [(walk[i], walk[(i + 1) % groups]) for i in range(groups)]
    back = [(b, a) for a, b in ahead]
    me = lax.axis_index("expert").astype(jnp.int32)
    after = jnp.where(me == groups - 1, 0, me + 1)
    place = jnp.stack([me, after, replica_pick[0]])
    weights = w_gate, w_up, w_down.reshape(-1, width)
    run = functools.partial(experts, place, weights, slots, height)

    first_a, first_b = pack(tokens, target, router_weight, slots)
    far = groups // 2
    a_left, b_left, a_right, b_right = first_a, first_b, first_a, first_b
    parts = {}
    own = run(first_a, first_a, 0), run(first_b, first_a, half)
    for s in range(1, far):
        a_left = lax.ppermute(a_left, "expert", ahead)
        b_right = lax.ppermute(b_right, "expert", back)
        a_right = lax.ppermute(a_right, "expert", back)
        b_left = lax.ppermute(b_left, "expert", ahead)
        parts[s] = run(a_left, a_left, 0), run(b_left, a_left, half), run(a_right, a_right, 0), run(b_right, a_right, half)
    a_left = lax.ppermute(a_left, "expert", ahead)
    b_right = lax.ppermute(b_right, "expert", back)
    far_a, far_b = run(a_left, a_left, 0), run(b_right, a_left, half)

    a_to_left = lax.ppermute(far_a, "expert", back)
    b_to_right = lax.ppermute(far_b, "expert", ahead)
    a_to_right = b_to_left = None
    for s in range(far - 1, 0, -1):
        pa_left, pb_left, pa_right, pb_right = parts[s]
        a_to_left = lax.ppermute(add(pa_left, a_to_left), "expert", back)
        b_to_right = lax.ppermute(add(pb_right, b_to_right), "expert", ahead)
        a_to_right = lax.ppermute(pa_right if a_to_right is None else add(pa_right, a_to_right), "expert", ahead)
        b_to_left = lax.ppermute(pb_left if b_to_left is None else add(pb_left, b_to_left), "expert", back)

    return finish((own[0], a_to_left, a_to_right), (own[1], b_to_left, b_to_right))


def solution(mesh):
    in_specs = (
        P(("dp", "expert"), None),
        P(("dp", "expert"), None),
        P(("dp", "expert"), None),
        P(("dp", "expert")),
        P("expert", None, None),
        P("expert", None, None),
        P("expert", None, None),
    )
    out_specs = P(("dp", "expert"), None)
    return jax.shard_map(body, mesh=mesh, in_specs=in_specs, out_specs=out_specs, check_vma=False)
```

```python
import functools

import jax
import jax.numpy as jnp
from jax import lax
from jax.experimental import pallas as pl
from jax.experimental.pallas import tpu as pltpu
from jax.sharding import PartitionSpec as P

VMEM_LIMIT = 12 * 1024 * 1024
PACK_LIMIT = 56 * 1024 * 1024


def ring_order(groups):
    columns = 1 << ((groups.bit_length() - 1) // 2)
    rows = groups // columns
    walk = [z * columns for z in range(rows)]
    for turn, z in enumerate(reversed(range(rows))):
        row = [z * columns + x for x in range(1, columns)]
        walk += row if turn % 2 == 0 else row[::-1]
    return walk


def table_rows(slots, height, width):
    one = -(-slots * height // width)
    return one, -(-2 * one // 8) * 8


def pack_kernel(slots, tokens_ref, target_ref, weight_ref, *refs):
    tabled, plain = refs[:2], refs[2:4]
    target_buf, weight_buf, sems = refs[4:]
    height, width = tokens_ref.shape
    half = height // 2
    one, extra = table_rows(slots, height, width)
    per_row = width // height
    copies = [
        pltpu.make_async_copy(target_ref, target_buf, sems.at[0]),
        pltpu.make_async_copy(weight_ref, weight_buf, sems.at[1]),
    ]
    for i in range(2):
        rows = tokens_ref.at[pl.ds(i * half, half)]
        copies.append(pltpu.make_async_copy(rows, tabled[i].at[pl.ds(0, half)], sems.at[2 + i]))
        copies.append(pltpu.make_async_copy(rows, plain[i], sems.at[4 + i]))
    for copy in copies:
        copy.start()
    copies[0].wait()
    copies[1].wait()
    weight = weight_buf[...]
    share = weight / jnp.sum(weight, axis=0, keepdims=True)
    target = target_buf[...]
    row = lax.broadcasted_iota(jnp.int32, (extra, height), 0)
    for lane in range(per_row):
        block = jnp.zeros((extra, height), jnp.float32)
        for r in range(one):
            slot = r * per_row + lane
            if slot < slots:
                value = jnp.sum(jnp.where(target == slot, share, 0.0), axis=0, keepdims=True)
                high = value.astype(jnp.bfloat16).astype(jnp.float32)
                block = jnp.where(row == r, high, block)
                block = jnp.where(row == one + r, value - high, block)
        for ref in tabled:
            ref[half:, lane * height:(lane + 1) * height] = block.astype(jnp.bfloat16)
    for copy in copies[2:]:
        copy.wait()


def pack(tokens, target, router_weight, slots):
    height, width = tokens.shape
    half, top = height // 2, target.shape[1]
    extra = table_rows(slots, height, width)[1]
    vmem = pl.BlockSpec(memory_space=pltpu.VMEM)
    return pl.pallas_call(
        functools.partial(pack_kernel, slots),
        in_specs=[pl.BlockSpec(memory_space=pl.ANY)] * 3,
        out_specs=[vmem] * 4,
        out_shape=[jax.ShapeDtypeStruct((half + extra, width), jnp.bfloat16)] * 2
        + [jax.ShapeDtypeStruct((half, width), jnp.bfloat16)] * 2,
        scratch_shapes=[
            pltpu.VMEM((top, height), jnp.int32),
            pltpu.VMEM((top, height), jnp.float32),
            pltpu.SemaphoreType.DMA((6,)),
        ],
        compiler_params=pltpu.CompilerParams(vmem_limit_bytes=PACK_LIMIT),
        cost_estimate=pl.CostEstimate(flops=0, bytes_accessed=4 * height * width, transcendentals=0),
    )(tokens, target.T, router_weight.T)


def columns(place_ref, table_ref, first, slots, height, owned):
    half = height // 2
    width = table_ref.shape[1]
    one, extra = table_rows(slots, height, width)
    per_row = width // height
    me, after, pick = place_ref[0], place_ref[1], place_ref[2]

    def column(slot):
        lane = pl.multiple_of(lax.rem(slot, per_row) * height + first, half)
        block = table_ref[half:half + extra, pl.ds(lane, half)].astype(jnp.float32)
        row = lax.broadcasted_iota(jnp.int32, block.shape, 0)
        line = lax.div(slot, per_row)
        return jnp.sum(jnp.where((row == line) | (row == one + line), block, 0.0), axis=0, keepdims=True)

    lent = column(after * (owned + 1) + owned)
    row = lax.broadcasted_iota(jnp.int32, (128, half), 0)
    shares = jnp.zeros((128, half), jnp.float32)
    for e in range(owned):
        line = column(me * (owned + 1) + e) + jnp.where(pick == e, lent, 0.0)
        shares = jnp.where(row == e, line, shares)
    return shares.T


def evaluate(chunk_ref, share_ref, gate_ref, up_ref, down_ref, out_ref, hidden_ref):
    half, width = out_ref.shape
    owned, _, units = gate_ref.shape
    tile = 256 if units % 256 == 0 else units
    tiles = units // tile
    wide = 512 if width % 512 == 0 else width

    def project(j, carry):
        e = lax.div(j, tiles)
        at = pl.ds(pl.multiple_of(lax.rem(j, tiles) * tile, tile), tile)
        x = chunk_ref[:half, :]
        gate = jnp.dot(x, gate_ref[e, :, at], preferred_element_type=jnp.float32)
        upper = jnp.dot(x, up_ref[e, :, at], preferred_element_type=jnp.float32)
        shares = share_ref[...]
        lane = lax.broadcasted_iota(jnp.int32, shares.shape, 1)
        share = jnp.sum(jnp.where(lane == e, shares, 0.0), axis=1, keepdims=True)
        hidden = gate / (1.0 + jnp.exp(-gate)) * upper * share
        hidden_ref[:, pl.ds(pl.multiple_of(j * tile, tile), tile)] = hidden.astype(jnp.bfloat16)
        return carry

    lax.fori_loop(0, owned * tiles, project, 0)

    def fold(j, carry):
        at = pl.ds(pl.multiple_of(j * wide, wide), wide)
        part = jnp.dot(hidden_ref[...], down_ref[:, at], preferred_element_type=jnp.float32)
        out_ref[:, at] = part.astype(jnp.bfloat16)
        return carry

    lax.fori_loop(0, width // wide, fold, 0)


def tabled_kernel(firsts, slots, height, place_ref, chunk_ref, gate_ref, up_ref, down_ref, out_ref, other_ref,
                  share_ref, hidden_ref):
    owned = gate_ref.shape[0]
    share_ref[...] = columns(place_ref, chunk_ref, firsts[0], slots, height, owned)
    other_ref[...] = columns(place_ref, chunk_ref, firsts[1], slots, height, owned)
    evaluate(chunk_ref, share_ref, gate_ref, up_ref, down_ref, out_ref, hidden_ref)


def plain_kernel(chunk_ref, share_ref, gate_ref, up_ref, down_ref, out_ref, same_ref, hidden_ref):
    del same_ref
    evaluate(chunk_ref, share_ref, gate_ref, up_ref, down_ref, out_ref, hidden_ref)


def cost(half, w_gate):
    owned, width, units = w_gate.shape
    return pl.CostEstimate(
        flops=6 * half * width * units * owned, bytes_accessed=8 * half * width, transcendentals=half * units * owned
    )


def tabled(place, weights, slots, height, firsts, chunk):
    half, (owned, width, units) = height // 2, weights[0].shape
    vmem = pl.BlockSpec(memory_space=pltpu.VMEM)
    return pl.pallas_call(
        functools.partial(tabled_kernel, firsts, slots, height),
        in_specs=[pl.BlockSpec(memory_space=pltpu.SMEM)] + [vmem] * 4,
        out_specs=[vmem, vmem],
        out_shape=[jax.ShapeDtypeStruct((half, width), jnp.bfloat16), jax.ShapeDtypeStruct((half, 128), jnp.float32)],
        scratch_shapes=[pltpu.VMEM((half, 128), jnp.float32), pltpu.VMEM((half, owned * units), jnp.bfloat16)],
        compiler_params=pltpu.CompilerParams(vmem_limit_bytes=VMEM_LIMIT),
        cost_estimate=cost(half, weights[0]),
    )(place, chunk, *weights)


def plain(weights, chunk, shares):
    (half, width), (owned, _, units) = chunk.shape, weights[0].shape
    vmem = pl.BlockSpec(memory_space=pltpu.VMEM)
    return pl.pallas_call(
        plain_kernel,
        in_specs=[vmem] * 5,
        out_specs=[vmem, vmem],
        out_shape=[jax.ShapeDtypeStruct((half, width), jnp.bfloat16)] * 2,
        scratch_shapes=[pltpu.VMEM((half, owned * units), jnp.bfloat16)],
        input_output_aliases={0: 1},
        compiler_params=pltpu.CompilerParams(vmem_limit_bytes=VMEM_LIMIT),
        cost_estimate=cost(half, weights[0]),
    )(chunk, shares, *weights)


def finish_kernel(*refs):
    out_ref = refs[-1]
    half = refs[0].shape[0]
    for i in range(2):
        total = sum(ref[...].astype(jnp.float32) for ref in refs[3 * i:3 * i + 3])
        out_ref[i * half:(i + 1) * half, :] = total.astype(out_ref.dtype)


def finish(a, b):
    half, width = a[0].shape
    vmem = pl.BlockSpec(memory_space=pltpu.VMEM)
    return pl.pallas_call(
        finish_kernel,
        in_specs=[vmem] * 6,
        out_specs=vmem,
        out_shape=jax.ShapeDtypeStruct((2 * half, width), a[0].dtype),
        compiler_params=pltpu.CompilerParams(vmem_limit_bytes=VMEM_LIMIT),
    )(*a, *b)


def add(a, b):
    return (a.astype(jnp.float32) + b.astype(jnp.float32)).astype(jnp.bfloat16)


def body(tokens, target, router_weight, replica_pick, w_gate, w_up, w_down):
    height, width = tokens.shape
    half = height // 2
    groups = lax.axis_size("expert")
    slots = groups * (w_gate.shape[0] + 1)
    walk = ring_order(groups)
    ahead = [(walk[i], walk[(i + 1) % groups]) for i in range(groups)]
    back = [(b, a) for a, b in ahead]
    me = lax.axis_index("expert").astype(jnp.int32)
    after = jnp.where(me == groups - 1, 0, me + 1)
    place = jnp.stack([me, after, replica_pick[0]])
    weights = w_gate, w_up, w_down.reshape(-1, width)
    far = groups // 2

    lead_a, lead_b, a, b = pack(tokens, target, router_weight, slots)
    run_a = functools.partial(tabled, place, weights, slots, height, (0, half))
    run_b = functools.partial(tabled, place, weights, slots, height, (half, 0))
    own_a, shares_b = run_a(lead_a)
    own_b, _ = plain(weights, b, shares_b)
    parts = {}
    for s in range(1, far):
        lead_a = lax.ppermute(lead_a, "expert", ahead)
        lead_b = lax.ppermute(lead_b, "expert", back)
        b = lax.ppermute(b, "expert", ahead)
        a = lax.ppermute(a, "expert", back)
        lead_part_a, shares_b = run_a(lead_a)
        lead_part_b, shares_a = run_b(lead_b)
        part_b, b = plain(weights, b, shares_b)
        part_a, a = plain(weights, a, shares_a)
        parts[s] = lead_part_a, lead_part_b, part_b, part_a
    far_a = run_a(lax.ppermute(lead_a, "expert", ahead))[0]
    far_b = run_b(lax.ppermute(lead_b, "expert", back))[0]

    lead_a, lead_b, a, b = lax.ppermute(far_a, "expert", back), lax.ppermute(far_b, "expert", ahead), None, None
    for s in range(far - 1, 0, -1):
        lead_part_a, lead_part_b, part_b, part_a = parts[s]
        b = lax.ppermute(part_b if b is None else add(part_b, b), "expert", back)
        a = lax.ppermute(part_a if a is None else add(part_a, a), "expert", ahead)
        lead_a = lax.ppermute(add(lead_part_a, lead_a), "expert", back)
        lead_b = lax.ppermute(add(lead_part_b, lead_b), "expert", ahead)
    return finish((own_a, a, lead_a), (own_b, b, lead_b))


def solution(mesh):
    in_specs = (
        P(("dp", "expert"), None),
        P(("dp", "expert"), None),
        P(("dp", "expert"), None),
        P(("dp", "expert")),
        P("expert", None, None),
        P("expert", None, None),
        P("expert", None, None),
    )
    out_specs = P(("dp", "expert"), None)
    return jax.shard_map(body, mesh=mesh, in_specs=in_specs, out_specs=out_specs, check_vma=False)
```

```python
import functools

import jax
import jax.numpy as jnp
from jax import lax
from jax.experimental import pallas as pl
from jax.experimental.pallas import tpu as pltpu
from jax.sharding import PartitionSpec as P

VMEM_LIMIT = 12 * 1024 * 1024
PACK_LIMIT = 56 * 1024 * 1024


def ring_order(groups):
    columns = 1 << ((groups.bit_length() - 1) // 2)
    rows = groups // columns
    walk = [z * columns for z in range(rows)]
    for turn, z in enumerate(reversed(range(rows))):
        row = [z * columns + x for x in range(1, columns)]
        walk += row if turn % 2 == 0 else row[::-1]
    return walk


def table_rows(slots, height, width):
    one = -(-slots * height // width)
    return one, -(-2 * one // 8) * 8


def pack_kernel(slots, tokens_ref, target_ref, weight_ref, *refs):
    tabled, plain = refs[:2], refs[2:4]
    target_buf, weight_buf, sems = refs[4:]
    height, width = tokens_ref.shape
    half = height // 2
    one, extra = table_rows(slots, height, width)
    per_row = width // height
    copies = [
        pltpu.make_async_copy(target_ref, target_buf, sems.at[0]),
        pltpu.make_async_copy(weight_ref, weight_buf, sems.at[1]),
    ]
    for i in range(2):
        rows = tokens_ref.at[pl.ds(i * half, half)]
        copies.append(pltpu.make_async_copy(rows, tabled[i].at[pl.ds(0, half)], sems.at[2 + i]))
        copies.append(pltpu.make_async_copy(rows, plain[i], sems.at[4 + i]))
    for copy in copies:
        copy.start()
    copies[0].wait()
    copies[1].wait()
    weight = weight_buf[...]
    share = weight / jnp.sum(weight, axis=0, keepdims=True)
    target = target_buf[...]
    row = lax.broadcasted_iota(jnp.int32, (extra, height), 0)
    for lane in range(per_row):
        block = jnp.zeros((extra, height), jnp.float32)
        for r in range(one):
            slot = r * per_row + lane
            if slot < slots:
                value = jnp.sum(jnp.where(target == slot, share, 0.0), axis=0, keepdims=True)
                high = value.astype(jnp.bfloat16).astype(jnp.float32)
                block = jnp.where(row == r, high, block)
                block = jnp.where(row == one + r, value - high, block)
        for ref in tabled:
            ref[half:, lane * height:(lane + 1) * height] = block.astype(jnp.bfloat16)
    for copy in copies[2:]:
        copy.wait()


def pack(tokens, target, router_weight, slots):
    height, width = tokens.shape
    half, top = height // 2, target.shape[1]
    extra = table_rows(slots, height, width)[1]
    vmem = pl.BlockSpec(memory_space=pltpu.VMEM)
    return pl.pallas_call(
        functools.partial(pack_kernel, slots),
        in_specs=[pl.BlockSpec(memory_space=pl.ANY)] * 3,
        out_specs=[vmem] * 4,
        out_shape=[jax.ShapeDtypeStruct((half + extra, width), jnp.bfloat16)] * 2
        + [jax.ShapeDtypeStruct((half, width), jnp.bfloat16)] * 2,
        scratch_shapes=[
            pltpu.VMEM((top, height), jnp.int32),
            pltpu.VMEM((top, height), jnp.float32),
            pltpu.SemaphoreType.DMA((6,)),
        ],
        compiler_params=pltpu.CompilerParams(vmem_limit_bytes=PACK_LIMIT),
        cost_estimate=pl.CostEstimate(flops=0, bytes_accessed=4 * height * width, transcendentals=0),
    )(tokens, target.T, router_weight.T)


def columns(place_ref, table_ref, first, slots, height, owned):
    half = height // 2
    width = table_ref.shape[1]
    one, extra = table_rows(slots, height, width)
    per_row = width // height
    me, after, pick = place_ref[0], place_ref[1], place_ref[2]

    def column(slot):
        lane = pl.multiple_of(lax.rem(slot, per_row) * height + first, half)
        block = table_ref[half:half + extra, pl.ds(lane, half)].astype(jnp.float32)
        row = lax.broadcasted_iota(jnp.int32, block.shape, 0)
        line = lax.div(slot, per_row)
        return jnp.sum(jnp.where((row == line) | (row == one + line), block, 0.0), axis=0, keepdims=True)

    lent = column(after * (owned + 1) + owned)
    row = lax.broadcasted_iota(jnp.int32, (128, half), 0)
    shares = jnp.zeros((128, half), jnp.float32)
    for e in range(owned):
        line = column(me * (owned + 1) + e) + jnp.where(pick == e, lent, 0.0)
        shares = jnp.where(row == e, line, shares)
    return shares.T


def evaluate(rows_ref, share_ref, gate_ref, up_ref, down_ref, outs, hidden_ref):
    half, width = outs[0].shape
    owned, _, units = gate_ref.shape
    wide = width // 2 if width % 256 == 0 else width

    def project(e, carry):
        x = rows_ref[...]
        gate = jnp.dot(x, gate_ref[e], preferred_element_type=jnp.float32)
        upper = jnp.dot(x, up_ref[e], preferred_element_type=jnp.float32)
        shares = share_ref[...]
        lane = lax.broadcasted_iota(jnp.int32, shares.shape, 1)
        share = jnp.sum(jnp.where(lane == e, shares, 0.0), axis=1, keepdims=True)
        hidden = gate / (1.0 + jnp.exp(-gate)) * upper * share
        hidden_ref[:, pl.ds(pl.multiple_of(e * units, units), units)] = hidden.astype(jnp.bfloat16)
        return carry

    lax.fori_loop(0, owned, project, 0)

    def fold(j, carry):
        at = pl.ds(pl.multiple_of(j * wide, wide), wide)
        part = jnp.dot(hidden_ref[...], down_ref[:, at], preferred_element_type=jnp.float32)
        for i, out_ref in enumerate(outs):
            out_ref[:, at] = part[i * half:(i + 1) * half].astype(jnp.bfloat16)
        return carry

    lax.fori_loop(0, width // wide, fold, 0)


def lead_kernel(slots, height, place_ref, a_ref, b_ref, gate_ref, up_ref, down_ref, *refs):
    out_a_ref, out_b_ref, other_ref, rows_ref, share_ref, hidden_ref = refs[-6:]
    owned = gate_ref.shape[0]
    half = height // 2
    for i, (ref, first) in enumerate(((a_ref, 0), (b_ref, half))):
        at = slice(i * half, (i + 1) * half)
        rows_ref[at, :] = ref[:half, :]
        share_ref[at, :] = columns(place_ref, ref, first, slots, height, owned)
        other_ref[at, :] = columns(place_ref, ref, half - first, slots, height, owned)
    evaluate(rows_ref, share_ref, gate_ref, up_ref, down_ref, (out_a_ref, out_b_ref), hidden_ref)


def plain_kernel(b_ref, a_ref, share_ref, gate_ref, up_ref, down_ref, out_b_ref, out_a_ref, same_b_ref, same_a_ref,
                 rows_ref, hidden_ref):
    del same_b_ref, same_a_ref
    half = b_ref.shape[0]
    rows_ref[:half, :] = b_ref[...]
    rows_ref[half:, :] = a_ref[...]
    evaluate(rows_ref, share_ref, gate_ref, up_ref, down_ref, (out_b_ref, out_a_ref), hidden_ref)


def cost(rows, w_gate):
    owned, width, units = w_gate.shape
    return pl.CostEstimate(
        flops=6 * rows * width * units * owned, bytes_accessed=8 * rows * width, transcendentals=rows * units * owned
    )


def lead(place, weights, slots, height, a, b, earlier=()):
    half, (owned, width, units) = height // 2, weights[0].shape
    vmem = pl.BlockSpec(memory_space=pltpu.VMEM)
    return pl.pallas_call(
        functools.partial(lead_kernel, slots, height),
        in_specs=[pl.BlockSpec(memory_space=pltpu.SMEM)] + [vmem] * 5 + [pl.BlockSpec(memory_space=pl.ANY)] * len(earlier),
        out_specs=[vmem] * 3,
        out_shape=[jax.ShapeDtypeStruct((half, width), jnp.bfloat16)] * 2
        + [jax.ShapeDtypeStruct((height, 128), jnp.float32)],
        scratch_shapes=[
            pltpu.VMEM((height, width), jnp.bfloat16),
            pltpu.VMEM((height, 128), jnp.float32),
            pltpu.VMEM((height, owned * units), jnp.bfloat16),
        ],
        compiler_params=pltpu.CompilerParams(vmem_limit_bytes=VMEM_LIMIT),
        cost_estimate=cost(height, weights[0]),
    )(place, a, b, *weights, *earlier)


def plain(weights, b, a, shares):
    (half, width), (owned, _, units) = b.shape, weights[0].shape
    vmem = pl.BlockSpec(memory_space=pltpu.VMEM)
    return pl.pallas_call(
        plain_kernel,
        in_specs=[vmem] * 6,
        out_specs=[vmem] * 4,
        out_shape=[jax.ShapeDtypeStruct((half, width), jnp.bfloat16)] * 4,
        scratch_shapes=[
            pltpu.VMEM((2 * half, width), jnp.bfloat16),
            pltpu.VMEM((2 * half, owned * units), jnp.bfloat16),
        ],
        input_output_aliases={0: 2, 1: 3},
        compiler_params=pltpu.CompilerParams(vmem_limit_bytes=VMEM_LIMIT),
        cost_estimate=cost(2 * half, weights[0]),
    )(b, a, shares, *weights)


def finish_kernel(*refs):
    out_ref = refs[-1]
    half = refs[0].shape[0]
    for i in range(2):
        total = sum(ref[...].astype(jnp.float32) for ref in refs[3 * i:3 * i + 3])
        out_ref[i * half:(i + 1) * half, :] = total.astype(out_ref.dtype)


def finish(a, b):
    half, width = a[0].shape
    vmem = pl.BlockSpec(memory_space=pltpu.VMEM)
    return pl.pallas_call(
        finish_kernel,
        in_specs=[vmem] * 6,
        out_specs=vmem,
        out_shape=jax.ShapeDtypeStruct((2 * half, width), a[0].dtype),
        compiler_params=pltpu.CompilerParams(vmem_limit_bytes=VMEM_LIMIT),
    )(*a, *b)


def add(a, b):
    return (a.astype(jnp.float32) + b.astype(jnp.float32)).astype(jnp.bfloat16)


def body(tokens, target, router_weight, replica_pick, w_gate, w_up, w_down):
    height, width = tokens.shape
    half = height // 2
    groups = lax.axis_size("expert")
    slots = groups * (w_gate.shape[0] + 1)
    walk = ring_order(groups)
    ahead = [(walk[i], walk[(i + 1) % groups]) for i in range(groups)]
    back = [(b, a) for a, b in ahead]
    me = lax.axis_index("expert").astype(jnp.int32)
    after = jnp.where(me == groups - 1, 0, me + 1)
    place = jnp.stack([me, after, replica_pick[0]])
    weights = w_gate, w_up, w_down.reshape(-1, width)
    far = groups // 2

    lead_a, lead_b, a, b = pack(tokens, target, router_weight, slots)
    run = functools.partial(lead, place, weights, slots, height)
    own_a, own_b, shares = run(lead_a, lead_b)
    earlier = (shares,)
    parts = {}
    for s in range(1, far):
        lead_a = lax.ppermute(lead_a, "expert", ahead)
        lead_b = lax.ppermute(lead_b, "expert", back)
        b = lax.ppermute(b, "expert", ahead)
        a = lax.ppermute(a, "expert", back)
        lead_part_a, lead_part_b, shares = run(lead_a, lead_b, earlier)
        part_b, part_a, b, a = plain(weights, b, a, shares)
        earlier = ()
        parts[s] = lead_part_a, lead_part_b, part_b, part_a
    far_a, far_b, _ = run(lax.ppermute(lead_a, "expert", ahead), lax.ppermute(lead_b, "expert", back))

    lead_a, lead_b, a, b = lax.ppermute(far_a, "expert", back), lax.ppermute(far_b, "expert", ahead), None, None
    for s in range(far - 1, 0, -1):
        lead_part_a, lead_part_b, part_b, part_a = parts[s]
        b = lax.ppermute(part_b if b is None else add(part_b, b), "expert", back)
        a = lax.ppermute(part_a if a is None else add(part_a, a), "expert", ahead)
        lead_a = lax.ppermute(add(lead_part_a, lead_a), "expert", back)
        lead_b = lax.ppermute(add(lead_part_b, lead_b), "expert", ahead)
    return finish((own_a, lead_a, a), (own_b, lead_b, b))


def solution(mesh):
    in_specs = (
        P(("dp", "expert"), None),
        P(("dp", "expert"), None),
        P(("dp", "expert"), None),
        P(("dp", "expert")),
        P("expert", None, None),
        P("expert", None, None),
        P("expert", None, None),
    )
    out_specs = P(("dp", "expert"), None)
    return jax.shard_map(body, mesh=mesh, in_specs=in_specs, out_specs=out_specs, check_vma=False)
```

```python
import functools

import jax
import jax.numpy as jnp
from jax import lax
from jax.experimental import pallas as pl
from jax.experimental.pallas import tpu as pltpu
from jax.sharding import PartitionSpec as P

VMEM_LIMIT = 12 * 1024 * 1024
SPLIT_LIMIT = 56 * 1024 * 1024
PACK_LIMIT = 40 * 1024 * 1024


def ring_order(groups):
    columns = 1 << ((groups.bit_length() - 1) // 2)
    rows = groups // columns
    walk = [z * columns for z in range(rows)]
    for turn, z in enumerate(reversed(range(rows))):
        row = [z * columns + x for x in range(1, columns)]
        walk += row if turn % 2 == 0 else row[::-1]
    return walk


def table_rows(slots, height, width):
    one = -(-slots * height // width)
    return one, -(-2 * one // 8) * 8


def split_kernel(tokens_ref, a_ref, b_ref, sems):
    half = a_ref.shape[0]
    copies = [
        pltpu.make_async_copy(tokens_ref.at[pl.ds(i * half, half)], ref, sems.at[i]) for i, ref in enumerate((a_ref, b_ref))
    ]
    for copy in copies:
        copy.start()
    for copy in copies:
        copy.wait()


def split(tokens):
    height, width = tokens.shape
    anywhere = pl.BlockSpec(memory_space=pl.ANY)
    return pl.pallas_call(
        split_kernel,
        in_specs=[anywhere],
        out_specs=[anywhere] * 2,
        out_shape=[jax.ShapeDtypeStruct((height // 2, width), jnp.bfloat16)] * 2,
        scratch_shapes=[pltpu.SemaphoreType.DMA((2,))],
        compiler_params=pltpu.CompilerParams(vmem_limit_bytes=SPLIT_LIMIT),
        cost_estimate=pl.CostEstimate(flops=0, bytes_accessed=4 * height * width, transcendentals=0),
    )(tokens)


def pack_kernel(slots, a_ref, b_ref, target_ref, weight_ref, *refs):
    tabled = refs[:2]
    target_buf, weight_buf, sems = refs[2:]
    half, width = a_ref.shape
    height = 2 * half
    one, extra = table_rows(slots, height, width)
    per_row = width // height
    copies = [
        pltpu.make_async_copy(target_ref, target_buf, sems.at[0]),
        pltpu.make_async_copy(weight_ref, weight_buf, sems.at[1]),
        pltpu.make_async_copy(a_ref, tabled[0].at[pl.ds(0, half)], sems.at[2]),
        pltpu.make_async_copy(b_ref, tabled[1].at[pl.ds(0, half)], sems.at[3]),
    ]
    for copy in copies:
        copy.start()
    copies[0].wait()
    copies[1].wait()
    weight = weight_buf[...]
    share = weight / jnp.sum(weight, axis=0, keepdims=True)
    target = target_buf[...]
    row = lax.broadcasted_iota(jnp.int32, (extra, height), 0)
    for lane in range(per_row):
        block = jnp.zeros((extra, height), jnp.float32)
        for r in range(one):
            slot = r * per_row + lane
            if slot < slots:
                value = jnp.sum(jnp.where(target == slot, share, 0.0), axis=0, keepdims=True)
                high = value.astype(jnp.bfloat16).astype(jnp.float32)
                block = jnp.where(row == r, high, block)
                block = jnp.where(row == one + r, value - high, block)
        for ref in tabled:
            ref[half:, lane * height:(lane + 1) * height] = block.astype(jnp.bfloat16)
    for copy in copies[2:]:
        copy.wait()


def pack(a, b, target, router_weight, slots):
    half, width = a.shape
    height, top = target.shape
    extra = table_rows(slots, height, width)[1]
    vmem = pl.BlockSpec(memory_space=pltpu.VMEM)
    return pl.pallas_call(
        functools.partial(pack_kernel, slots),
        in_specs=[pl.BlockSpec(memory_space=pl.ANY)] * 4,
        out_specs=[vmem] * 2,
        out_shape=[jax.ShapeDtypeStruct((half + extra, width), jnp.bfloat16)] * 2,
        scratch_shapes=[
            pltpu.VMEM((top, height), jnp.int32),
            pltpu.VMEM((top, height), jnp.float32),
            pltpu.SemaphoreType.DMA((4,)),
        ],
        compiler_params=pltpu.CompilerParams(vmem_limit_bytes=PACK_LIMIT),
        cost_estimate=pl.CostEstimate(flops=0, bytes_accessed=4 * height * width, transcendentals=0),
    )(a, b, target.T, router_weight.T)


def columns(place_ref, table_ref, first, slots, height, owned):
    half = height // 2
    width = table_ref.shape[1]
    one, extra = table_rows(slots, height, width)
    per_row = width // height
    me, after, pick = place_ref[0], place_ref[1], place_ref[2]

    def column(slot):
        lane = pl.multiple_of(lax.rem(slot, per_row) * height + first, half)
        block = table_ref[half:half + extra, pl.ds(lane, half)].astype(jnp.float32)
        row = lax.broadcasted_iota(jnp.int32, block.shape, 0)
        line = lax.div(slot, per_row)
        return jnp.sum(jnp.where((row == line) | (row == one + line), block, 0.0), axis=0, keepdims=True)

    lent = column(after * (owned + 1) + owned)
    row = lax.broadcasted_iota(jnp.int32, (128, half), 0)
    shares = jnp.zeros((128, half), jnp.float32)
    for e in range(owned):
        line = column(me * (owned + 1) + e) + jnp.where(pick == e, lent, 0.0)
        shares = jnp.where(row == e, line, shares)
    return shares.T


def evaluate(rows_ref, share_ref, gate_ref, up_ref, down_ref, outs, hidden_ref):
    half, width = outs[0].shape
    owned, _, units = gate_ref.shape
    wide = width // 2 if width % 256 == 0 else width

    def project(e, carry):
        x = rows_ref[...]
        gate = jnp.dot(x, gate_ref[e], preferred_element_type=jnp.float32)
        upper = jnp.dot(x, up_ref[e], preferred_element_type=jnp.float32)
        shares = share_ref[...]
        lane = lax.broadcasted_iota(jnp.int32, shares.shape, 1)
        share = jnp.sum(jnp.where(lane == e, shares, 0.0), axis=1, keepdims=True)
        hidden = gate / (1.0 + jnp.exp(-gate)) * upper * share
        hidden_ref[:, pl.ds(pl.multiple_of(e * units, units), units)] = hidden.astype(jnp.bfloat16)
        return carry

    lax.fori_loop(0, owned, project, 0)

    def fold(j, carry):
        at = pl.ds(pl.multiple_of(j * wide, wide), wide)
        part = jnp.dot(hidden_ref[...], down_ref[:, at], preferred_element_type=jnp.float32)
        for i, out_ref in enumerate(outs):
            out_ref[:, at] = part[i * half:(i + 1) * half].astype(jnp.bfloat16)
        return carry

    lax.fori_loop(0, width // wide, fold, 0)


def lead_kernel(slots, height, place_ref, a_ref, b_ref, gate_ref, up_ref, down_ref, *refs):
    out_a_ref, out_b_ref, other_ref, rows_ref, share_ref, hidden_ref = refs[-6:]
    owned = gate_ref.shape[0]
    half = height // 2
    for i, (ref, first) in enumerate(((a_ref, 0), (b_ref, half))):
        at = slice(i * half, (i + 1) * half)
        rows_ref[at, :] = ref[:half, :]
        share_ref[at, :] = columns(place_ref, ref, first, slots, height, owned)
        other_ref[at, :] = columns(place_ref, ref, half - first, slots, height, owned)
    evaluate(rows_ref, share_ref, gate_ref, up_ref, down_ref, (out_a_ref, out_b_ref), hidden_ref)


def plain_kernel(b_ref, a_ref, share_ref, gate_ref, up_ref, down_ref, out_b_ref, out_a_ref, same_b_ref, same_a_ref,
                 rows_ref, hidden_ref):
    del same_b_ref, same_a_ref
    half = b_ref.shape[0]
    rows_ref[:half, :] = b_ref[...]
    rows_ref[half:, :] = a_ref[...]
    evaluate(rows_ref, share_ref, gate_ref, up_ref, down_ref, (out_b_ref, out_a_ref), hidden_ref)


def cost(rows, w_gate):
    owned, width, units = w_gate.shape
    return pl.CostEstimate(
        flops=6 * rows * width * units * owned, bytes_accessed=8 * rows * width, transcendentals=rows * units * owned
    )


def lead(place, weights, slots, height, a, b, earlier=()):
    half, (owned, width, units) = height // 2, weights[0].shape
    vmem = pl.BlockSpec(memory_space=pltpu.VMEM)
    return pl.pallas_call(
        functools.partial(lead_kernel, slots, height),
        in_specs=[pl.BlockSpec(memory_space=pltpu.SMEM)] + [vmem] * 5 + [pl.BlockSpec(memory_space=pl.ANY)] * len(earlier),
        out_specs=[vmem] * 3,
        out_shape=[jax.ShapeDtypeStruct((half, width), jnp.bfloat16)] * 2
        + [jax.ShapeDtypeStruct((height, 128), jnp.float32)],
        scratch_shapes=[
            pltpu.VMEM((height, width), jnp.bfloat16),
            pltpu.VMEM((height, 128), jnp.float32),
            pltpu.VMEM((height, owned * units), jnp.bfloat16),
        ],
        compiler_params=pltpu.CompilerParams(vmem_limit_bytes=VMEM_LIMIT),
        cost_estimate=cost(height, weights[0]),
    )(place, a, b, *weights, *earlier)


def plain(weights, b, a, shares):
    (half, width), (owned, _, units) = b.shape, weights[0].shape
    vmem = pl.BlockSpec(memory_space=pltpu.VMEM)
    return pl.pallas_call(
        plain_kernel,
        in_specs=[vmem] * 6,
        out_specs=[vmem] * 4,
        out_shape=[jax.ShapeDtypeStruct((half, width), jnp.bfloat16)] * 4,
        scratch_shapes=[
            pltpu.VMEM((2 * half, width), jnp.bfloat16),
            pltpu.VMEM((2 * half, owned * units), jnp.bfloat16),
        ],
        input_output_aliases={0: 2, 1: 3},
        compiler_params=pltpu.CompilerParams(vmem_limit_bytes=VMEM_LIMIT),
        cost_estimate=cost(2 * half, weights[0]),
    )(b, a, shares, *weights)


def finish_kernel(index, own_ref, first_ref, last_ref, *refs):
    out_ref, total_ref, sem = refs[-3:]
    half = own_ref.shape[0]
    total = own_ref[...].astype(jnp.float32) + first_ref[...].astype(jnp.float32) + last_ref[...].astype(jnp.float32)
    total_ref[...] = total.astype(total_ref.dtype)
    copy = pltpu.make_async_copy(total_ref, out_ref.at[pl.ds(index * half, half)], sem)
    copy.start()
    copy.wait()


def finish(index, terms, out=()):
    half, width = terms[0].shape
    vmem, anywhere = pl.BlockSpec(memory_space=pltpu.VMEM), pl.BlockSpec(memory_space=pl.ANY)
    return pl.pallas_call(
        functools.partial(finish_kernel, index),
        in_specs=[vmem] * 3 + [anywhere] * len(out),
        out_specs=anywhere,
        out_shape=jax.ShapeDtypeStruct((2 * half, width), terms[0].dtype),
        scratch_shapes=[pltpu.VMEM((half, width), terms[0].dtype), pltpu.SemaphoreType.DMA],
        input_output_aliases={3: 0} if out else {},
        compiler_params=pltpu.CompilerParams(vmem_limit_bytes=VMEM_LIMIT),
    )(*terms, *out)


def add(a, b):
    return (a.astype(jnp.float32) + b.astype(jnp.float32)).astype(jnp.bfloat16)


def body(tokens, target, router_weight, replica_pick, w_gate, w_up, w_down):
    height, width = tokens.shape
    half = height // 2
    groups = lax.axis_size("expert")
    slots = groups * (w_gate.shape[0] + 1)
    walk = ring_order(groups)
    ahead = [(walk[i], walk[(i + 1) % groups]) for i in range(groups)]
    back = [(b, a) for a, b in ahead]
    me = lax.axis_index("expert").astype(jnp.int32)
    after = jnp.where(me == groups - 1, 0, me + 1)
    place = jnp.stack([me, after, replica_pick[0]])
    weights = w_gate, w_up, w_down.reshape(-1, width)
    far = groups // 2

    a, b = split(tokens)
    lead_a, lead_b = pack(a, b, target, router_weight, slots)
    run = functools.partial(lead, place, weights, slots, height)
    own_a, own_b, shares = run(lead_a, lead_b)
    earlier = (shares,)
    parts = {}
    for s in range(1, far):
        lead_a = lax.ppermute(lead_a, "expert", ahead)
        lead_b = lax.ppermute(lead_b, "expert", back)
        b = lax.ppermute(b, "expert", ahead)
        a = lax.ppermute(a, "expert", back)
        lead_part_a, lead_part_b, shares = run(lead_a, lead_b, earlier)
        part_b, part_a, b, a = plain(weights, b, a, shares)
        earlier = ()
        parts[s] = lead_part_a, lead_part_b, part_b, part_a
    far_a, far_b, _ = run(lax.ppermute(lead_a, "expert", ahead), lax.ppermute(lead_b, "expert", back))

    lead_a, lead_b, a, b = lax.ppermute(far_a, "expert", back), lax.ppermute(far_b, "expert", ahead), None, None
    for s in range(far - 1, 0, -1):
        lead_part_a, lead_part_b, part_b, part_a = parts[s]
        b = lax.ppermute(part_b if b is None else add(part_b, b), "expert", back)
        a = lax.ppermute(part_a if a is None else add(part_a, a), "expert", ahead)
        lead_a = lax.ppermute(add(lead_part_a, lead_a), "expert", back)
        lead_b = lax.ppermute(add(lead_part_b, lead_b), "expert", ahead)
    out = finish(0, (own_a, lead_a, a))
    return finish(1, (own_b, lead_b, b), (out,))


def solution(mesh):
    in_specs = (
        P(("dp", "expert"), None),
        P(("dp", "expert"), None),
        P(("dp", "expert"), None),
        P(("dp", "expert")),
        P("expert", None, None),
        P("expert", None, None),
        P("expert", None, None),
    )
    out_specs = P(("dp", "expert"), None)
    return jax.shard_map(body, mesh=mesh, in_specs=in_specs, out_specs=out_specs, check_vma=False)
```

```python
import functools

import jax
import jax.numpy as jnp
from jax import lax
from jax.experimental import pallas as pl
from jax.experimental.pallas import tpu as pltpu
from jax.sharding import PartitionSpec as P

VMEM_LIMIT = 12 * 1024 * 1024
PACK_LIMIT = 40 * 1024 * 1024


def ring_order(groups):
    columns = 1 << ((groups.bit_length() - 1) // 2)
    rows = groups // columns
    walk = [z * columns for z in range(rows)]
    for turn, z in enumerate(reversed(range(rows))):
        row = [z * columns + x for x in range(1, columns)]
        walk += row if turn % 2 == 0 else row[::-1]
    return walk


def table_rows(slots, height, width):
    one = -(-slots * height // width)
    return one, -(-2 * one // 8) * 8


def pack_kernel(slots, a_ref, b_ref, target_ref, weight_ref, *refs):
    tabled = refs[:2]
    target_buf, weight_buf, sems = refs[2:]
    half, width = a_ref.shape
    height = 2 * half
    one, extra = table_rows(slots, height, width)
    per_row = width // height
    copies = [
        pltpu.make_async_copy(target_ref, target_buf, sems.at[0]),
        pltpu.make_async_copy(weight_ref, weight_buf, sems.at[1]),
        pltpu.make_async_copy(a_ref, tabled[0].at[pl.ds(0, half)], sems.at[2]),
        pltpu.make_async_copy(b_ref, tabled[1].at[pl.ds(0, half)], sems.at[3]),
    ]
    for copy in copies:
        copy.start()
    copies[0].wait()
    copies[1].wait()
    weight = weight_buf[...]
    share = weight / jnp.sum(weight, axis=0, keepdims=True)
    target = target_buf[...]
    row = lax.broadcasted_iota(jnp.int32, (extra, height), 0)
    for lane in range(per_row):
        block = jnp.zeros((extra, height), jnp.float32)
        for r in range(one):
            slot = r * per_row + lane
            if slot < slots:
                value = jnp.sum(jnp.where(target == slot, share, 0.0), axis=0, keepdims=True)
                high = value.astype(jnp.bfloat16).astype(jnp.float32)
                block = jnp.where(row == r, high, block)
                block = jnp.where(row == one + r, value - high, block)
        for ref in tabled:
            ref[half:, lane * height:(lane + 1) * height] = block.astype(jnp.bfloat16)
    for copy in copies[2:]:
        copy.wait()


def pack(a, b, target, router_weight, slots):
    half, width = a.shape
    height, top = target.shape
    extra = table_rows(slots, height, width)[1]
    vmem = pl.BlockSpec(memory_space=pltpu.VMEM)
    return pl.pallas_call(
        functools.partial(pack_kernel, slots),
        in_specs=[pl.BlockSpec(memory_space=pl.ANY)] * 4,
        out_specs=[vmem] * 2,
        out_shape=[jax.ShapeDtypeStruct((half + extra, width), jnp.bfloat16)] * 2,
        scratch_shapes=[
            pltpu.VMEM((top, height), jnp.int32),
            pltpu.VMEM((top, height), jnp.float32),
            pltpu.SemaphoreType.DMA((4,)),
        ],
        compiler_params=pltpu.CompilerParams(vmem_limit_bytes=PACK_LIMIT),
        cost_estimate=pl.CostEstimate(flops=0, bytes_accessed=4 * height * width, transcendentals=0),
    )(a, b, target.T, router_weight.T)


def columns(place_ref, table_ref, first, slots, height, owned):
    half = height // 2
    width = table_ref.shape[1]
    one, extra = table_rows(slots, height, width)
    per_row = width // height
    me, after, pick = place_ref[0], place_ref[1], place_ref[2]

    def column(slot):
        lane = pl.multiple_of(lax.rem(slot, per_row) * height + first, half)
        block = table_ref[half:half + extra, pl.ds(lane, half)].astype(jnp.float32)
        row = lax.broadcasted_iota(jnp.int32, block.shape, 0)
        line = lax.div(slot, per_row)
        return jnp.sum(jnp.where((row == line) | (row == one + line), block, 0.0), axis=0, keepdims=True)

    lent = column(after * (owned + 1) + owned)
    row = lax.broadcasted_iota(jnp.int32, (128, half), 0)
    shares = jnp.zeros((128, half), jnp.float32)
    for e in range(owned):
        line = column(me * (owned + 1) + e) + jnp.where(pick == e, lent, 0.0)
        shares = jnp.where(row == e, line, shares)
    return shares.T


def evaluate(rows_ref, share_ref, gate_ref, up_ref, down_ref, outs, hidden_ref):
    half, width = outs[0].shape
    owned, _, units = gate_ref.shape
    wide = width // 2 if width % 256 == 0 else width

    def project(e, carry):
        x = rows_ref[...]
        gate = jnp.dot(x, gate_ref[e], preferred_element_type=jnp.float32)
        upper = jnp.dot(x, up_ref[e], preferred_element_type=jnp.float32)
        shares = share_ref[...]
        lane = lax.broadcasted_iota(jnp.int32, shares.shape, 1)
        share = jnp.sum(jnp.where(lane == e, shares, 0.0), axis=1, keepdims=True)
        hidden = gate / (1.0 + jnp.exp(-gate)) * upper * share
        hidden_ref[:, pl.ds(pl.multiple_of(e * units, units), units)] = hidden.astype(jnp.bfloat16)
        return carry

    lax.fori_loop(0, owned, project, 0)

    def fold(j, carry):
        at = pl.ds(pl.multiple_of(j * wide, wide), wide)
        part = jnp.dot(hidden_ref[...], down_ref[:, at], preferred_element_type=jnp.float32)
        for i, out_ref in enumerate(outs):
            out_ref[:, at] = part[i * half:(i + 1) * half].astype(jnp.bfloat16)
        return carry

    lax.fori_loop(0, width // wide, fold, 0)


def lead_kernel(slots, height, place_ref, a_ref, b_ref, gate_ref, up_ref, down_ref, *refs):
    out_a_ref, out_b_ref, other_ref, rows_ref, share_ref, hidden_ref = refs[-6:]
    owned = gate_ref.shape[0]
    half = height // 2
    for i, (ref, first) in enumerate(((a_ref, 0), (b_ref, half))):
        at = slice(i * half, (i + 1) * half)
        rows_ref[at, :] = ref[:half, :]
        share_ref[at, :] = columns(place_ref, ref, first, slots, height, owned)
        other_ref[at, :] = columns(place_ref, ref, half - first, slots, height, owned)
    evaluate(rows_ref, share_ref, gate_ref, up_ref, down_ref, (out_a_ref, out_b_ref), hidden_ref)


def plain_kernel(b_ref, a_ref, share_ref, gate_ref, up_ref, down_ref, out_b_ref, out_a_ref, same_b_ref, same_a_ref,
                 rows_ref, hidden_ref):
    same_b_ref[...] = b_ref[...]
    same_a_ref[...] = a_ref[...]
    half = b_ref.shape[0]
    rows_ref[:half, :] = b_ref[...]
    rows_ref[half:, :] = a_ref[...]
    evaluate(rows_ref, share_ref, gate_ref, up_ref, down_ref, (out_b_ref, out_a_ref), hidden_ref)


def cost(rows, w_gate):
    owned, width, units = w_gate.shape
    return pl.CostEstimate(
        flops=6 * rows * width * units * owned, bytes_accessed=8 * rows * width, transcendentals=rows * units * owned
    )


def lead(place, weights, slots, height, a, b, earlier=()):
    half, (owned, width, units) = height // 2, weights[0].shape
    vmem = pl.BlockSpec(memory_space=pltpu.VMEM)
    return pl.pallas_call(
        functools.partial(lead_kernel, slots, height),
        in_specs=[pl.BlockSpec(memory_space=pltpu.SMEM)] + [vmem] * 5 + [pl.BlockSpec(memory_space=pl.ANY)] * len(earlier),
        out_specs=[vmem] * 3,
        out_shape=[jax.ShapeDtypeStruct((half, width), jnp.bfloat16)] * 2
        + [jax.ShapeDtypeStruct((height, 128), jnp.float32)],
        scratch_shapes=[
            pltpu.VMEM((height, width), jnp.bfloat16),
            pltpu.VMEM((height, 128), jnp.float32),
            pltpu.VMEM((height, owned * units), jnp.bfloat16),
        ],
        compiler_params=pltpu.CompilerParams(vmem_limit_bytes=VMEM_LIMIT),
        cost_estimate=cost(height, weights[0]),
    )(place, a, b, *weights, *earlier)


def plain(weights, b, a, shares):
    (half, width), (owned, _, units) = b.shape, weights[0].shape
    vmem = pl.BlockSpec(memory_space=pltpu.VMEM)
    return pl.pallas_call(
        plain_kernel,
        in_specs=[vmem] * 6,
        out_specs=[vmem] * 4,
        out_shape=[jax.ShapeDtypeStruct((half, width), jnp.bfloat16)] * 4,
        scratch_shapes=[
            pltpu.VMEM((2 * half, width), jnp.bfloat16),
            pltpu.VMEM((2 * half, owned * units), jnp.bfloat16),
        ],
        compiler_params=pltpu.CompilerParams(vmem_limit_bytes=VMEM_LIMIT),
        cost_estimate=cost(2 * half, weights[0]),
    )(b, a, shares, *weights)


def finish_kernel(*refs):
    terms, (out_ref, total_ref, sems) = refs[:-3], refs[-3:]
    half = terms[0].shape[0]
    copies = []
    for i in range(2):
        rows = pl.ds(i * half, half)
        total = sum(ref[...].astype(jnp.float32) for ref in terms[3 * i:3 * i + 3])
        total_ref[rows, :] = total.astype(total_ref.dtype)
        copies.append(pltpu.make_async_copy(total_ref.at[rows], out_ref.at[rows], sems.at[i]))
        copies[i].start()
    for copy in copies:
        copy.wait()


def finish(a, b):
    half, width = a[0].shape
    return pl.pallas_call(
        finish_kernel,
        in_specs=[pl.BlockSpec(memory_space=pltpu.VMEM)] * 6,
        out_specs=pl.BlockSpec(memory_space=pl.ANY),
        out_shape=jax.ShapeDtypeStruct((2 * half, width), a[0].dtype),
        scratch_shapes=[pltpu.VMEM((2 * half, width), a[0].dtype), pltpu.SemaphoreType.DMA((2,))],
        compiler_params=pltpu.CompilerParams(vmem_limit_bytes=VMEM_LIMIT),
    )(*a, *b)


def add(a, b):
    return (a.astype(jnp.float32) + b.astype(jnp.float32)).astype(jnp.bfloat16)


def body(tokens, target, router_weight, replica_pick, w_gate, w_up, w_down):
    height, width = tokens.shape
    half = height // 2
    groups = lax.axis_size("expert")
    slots = groups * (w_gate.shape[0] + 1)
    walk = ring_order(groups)
    ahead = [(walk[i], walk[(i + 1) % groups]) for i in range(groups)]
    back = [(b, a) for a, b in ahead]
    me = lax.axis_index("expert").astype(jnp.int32)
    after = jnp.where(me == groups - 1, 0, me + 1)
    place = jnp.stack([me, after, replica_pick[0]])
    weights = w_gate, w_up, w_down.reshape(-1, width)
    far = groups // 2

    a, b = tokens[:half], tokens[half:]
    lead_a, lead_b = pack(a, b, target, router_weight, slots)
    run = functools.partial(lead, place, weights, slots, height)
    own_a, own_b, shares = run(lead_a, lead_b)
    earlier = (shares,)
    parts = {}
    for s in range(1, far):
        lead_a = lax.ppermute(lead_a, "expert", ahead)
        lead_b = lax.ppermute(lead_b, "expert", back)
        b = lax.ppermute(b, "expert", ahead)
        a = lax.ppermute(a, "expert", back)
        lead_part_a, lead_part_b, shares = run(lead_a, lead_b, earlier)
        part_b, part_a, b, a = plain(weights, b, a, shares)
        earlier = ()
        parts[s] = lead_part_a, lead_part_b, part_b, part_a
    far_a, far_b, _ = run(lax.ppermute(lead_a, "expert", ahead), lax.ppermute(lead_b, "expert", back))

    lead_a, lead_b, a, b = lax.ppermute(far_a, "expert", back), lax.ppermute(far_b, "expert", ahead), None, None
    for s in range(far - 1, 0, -1):
        lead_part_a, lead_part_b, part_b, part_a = parts[s]
        b = lax.ppermute(part_b if b is None else add(part_b, b), "expert", back)
        a = lax.ppermute(part_a if a is None else add(part_a, a), "expert", ahead)
        lead_a = lax.ppermute(add(lead_part_a, lead_a), "expert", back)
        lead_b = lax.ppermute(add(lead_part_b, lead_b), "expert", ahead)
    return finish((own_a, lead_a, a), (own_b, lead_b, b))


def solution(mesh):
    in_specs = (
        P(("dp", "expert"), None),
        P(("dp", "expert"), None),
        P(("dp", "expert"), None),
        P(("dp", "expert")),
        P("expert", None, None),
        P("expert", None, None),
        P("expert", None, None),
    )
    out_specs = P(("dp", "expert"), None)
    return jax.shard_map(body, mesh=mesh, in_specs=in_specs, out_specs=out_specs, check_vma=False)
```

```python
import functools

import jax
import jax.numpy as jnp
from jax import lax
from jax.experimental import pallas as pl
from jax.experimental.pallas import tpu as pltpu
from jax.sharding import PartitionSpec as P

VMEM_LIMIT = 12 * 1024 * 1024


def ring_order(groups):
    columns = 1 << ((groups.bit_length() - 1) // 2)
    rows = groups // columns
    walk = [z * columns for z in range(rows)]
    for turn, z in enumerate(reversed(range(rows))):
        row = [z * columns + x for x in range(1, columns)]
        walk += row if turn % 2 == 0 else row[::-1]
    return walk


def table_rows(slots):
    return -(-2 * slots // 16) * 16


def tiles(half, width):
    across = width // half
    for i in range(half // 16):
        for j in range(across):
            at = (i * across + j) * 16
            yield slice(i * 16, i * 16 + 16), slice(j * half, (j + 1) * half), slice(at, at + 16)


def pack_kernel(slots, a_ref, b_ref, target_ref, weight_ref, out_a_ref, out_b_ref):
    half, width = a_ref.shape
    for rows, columns, packed in tiles(half, width):
        out_a_ref[packed, :] = a_ref[rows, columns]
        out_b_ref[packed, :] = b_ref[rows, columns]
    weight = weight_ref[...]
    share = weight / jnp.sum(weight, axis=0, keepdims=True)
    target = target_ref[...]
    row = lax.broadcasted_iota(jnp.int32, (table_rows(slots), half), 0)
    block = jnp.zeros(row.shape, jnp.float32)
    for slot in range(slots):
        value = jnp.sum(jnp.where(target == slot, share, 0.0), axis=0, keepdims=True)
        block = jnp.where(row == slot, value[:, :half], block)
        block = jnp.where(row == slots + slot, value[:, half:], block)
    out_a_ref[width:, :] = block.astype(jnp.bfloat16)
    out_b_ref[width:, :] = block.astype(jnp.bfloat16)


def pack(a, b, target, router_weight, slots):
    half, width = a.shape
    vmem = pl.BlockSpec(memory_space=pltpu.VMEM)
    return pl.pallas_call(
        functools.partial(pack_kernel, slots),
        in_specs=[vmem] * 4,
        out_specs=[vmem] * 2,
        out_shape=[jax.ShapeDtypeStruct((width + table_rows(slots), half), jnp.bfloat16)] * 2,
        compiler_params=pltpu.CompilerParams(vmem_limit_bytes=VMEM_LIMIT),
        cost_estimate=pl.CostEstimate(flops=0, bytes_accessed=8 * half * width, transcendentals=0),
    )(a, b, target.T, router_weight.T)


def columns(place_ref, lead_ref, index, slots, owned):
    rows, half = lead_ref.shape
    extra = table_rows(slots)
    me, after, pick = place_ref[0], place_ref[1], place_ref[2]
    block = lead_ref[rows - extra:, :].astype(jnp.float32)
    row = lax.broadcasted_iota(jnp.int32, block.shape, 0)

    def column(slot):
        return jnp.sum(jnp.where(row == index * slots + slot, block, 0.0), axis=0, keepdims=True)

    lent = column(after * (owned + 1) + owned)
    line_of = lax.broadcasted_iota(jnp.int32, (128, half), 0)
    shares = jnp.zeros((128, half), jnp.float32)
    for e in range(owned):
        line = column(me * (owned + 1) + e) + jnp.where(pick == e, lent, 0.0)
        shares = jnp.where(line_of == e, line, shares)
    return shares.T


def evaluate(rows_ref, share_ref, gate_ref, up_ref, down_ref, outs, hidden_ref):
    half, width = outs[0].shape
    owned, _, units = gate_ref.shape
    wide = width // 2 if width % 256 == 0 else width

    def project(e, carry):
        x = rows_ref[...]
        gate = jnp.dot(x, gate_ref[e], preferred_element_type=jnp.float32)
        upper = jnp.dot(x, up_ref[e], preferred_element_type=jnp.float32)
        shares = share_ref[...]
        lane = lax.broadcasted_iota(jnp.int32, shares.shape, 1)
        share = jnp.sum(jnp.where(lane == e, shares, 0.0), axis=1, keepdims=True)
        hidden = gate / (1.0 + jnp.exp(-gate)) * upper * share
        hidden_ref[:, pl.ds(pl.multiple_of(e * units, units), units)] = hidden.astype(jnp.bfloat16)
        return carry

    lax.fori_loop(0, owned, project, 0)

    def fold(j, carry):
        at = pl.ds(pl.multiple_of(j * wide, wide), wide)
        part = jnp.dot(hidden_ref[...], down_ref[:, at], preferred_element_type=jnp.float32)
        for i, out_ref in enumerate(outs):
            out_ref[:, at] = part[i * half:(i + 1) * half].astype(jnp.bfloat16)
        return carry

    lax.fori_loop(0, width // wide, fold, 0)


def lead_kernel(slots, place_ref, a_ref, b_ref, gate_ref, up_ref, down_ref, *refs):
    out_a_ref, out_b_ref, other_ref, rows_ref, share_ref, hidden_ref = refs[-6:]
    owned = gate_ref.shape[0]
    half, width = out_a_ref.shape
    for i, ref in enumerate((a_ref, b_ref)):
        at = slice(i * half, (i + 1) * half)
        for rows, across, packed in tiles(half, width):
            rows_ref[i * half + rows.start:i * half + rows.stop, across] = ref[packed, :]
        share_ref[at, :] = columns(place_ref, ref, i, slots, owned)
        other_ref[at, :] = columns(place_ref, ref, 1 - i, slots, owned)
    evaluate(rows_ref, share_ref, gate_ref, up_ref, down_ref, (out_a_ref, out_b_ref), hidden_ref)


def plain_kernel(b_ref, a_ref, share_ref, gate_ref, up_ref, down_ref, out_b_ref, out_a_ref, same_b_ref, same_a_ref,
                 rows_ref, hidden_ref):
    same_b_ref[...] = b_ref[...]
    same_a_ref[...] = a_ref[...]
    half = b_ref.shape[0]
    rows_ref[:half, :] = b_ref[...]
    rows_ref[half:, :] = a_ref[...]
    evaluate(rows_ref, share_ref, gate_ref, up_ref, down_ref, (out_b_ref, out_a_ref), hidden_ref)


def cost(rows, w_gate):
    owned, width, units = w_gate.shape
    return pl.CostEstimate(
        flops=6 * rows * width * units * owned, bytes_accessed=8 * rows * width, transcendentals=rows * units * owned
    )


def lead(place, weights, slots, a, b, earlier=()):
    half, (owned, width, units) = a.shape[1], weights[0].shape
    height = 2 * half
    vmem = pl.BlockSpec(memory_space=pltpu.VMEM)
    return pl.pallas_call(
        functools.partial(lead_kernel, slots),
        in_specs=[pl.BlockSpec(memory_space=pltpu.SMEM)] + [vmem] * 5 + [pl.BlockSpec(memory_space=pl.ANY)] * len(earlier),
        out_specs=[vmem] * 3,
        out_shape=[jax.ShapeDtypeStruct((half, width), jnp.bfloat16)] * 2
        + [jax.ShapeDtypeStruct((height, 128), jnp.float32)],
        scratch_shapes=[
            pltpu.VMEM((height, width), jnp.bfloat16),
            pltpu.VMEM((height, 128), jnp.float32),
            pltpu.VMEM((height, owned * units), jnp.bfloat16),
        ],
        compiler_params=pltpu.CompilerParams(vmem_limit_bytes=VMEM_LIMIT),
        cost_estimate=cost(height, weights[0]),
    )(place, a, b, *weights, *earlier)


def plain(weights, b, a, shares):
    (half, width), (owned, _, units) = b.shape, weights[0].shape
    vmem = pl.BlockSpec(memory_space=pltpu.VMEM)
    return pl.pallas_call(
        plain_kernel,
        in_specs=[vmem] * 6,
        out_specs=[vmem] * 4,
        out_shape=[jax.ShapeDtypeStruct((half, width), jnp.bfloat16)] * 4,
        scratch_shapes=[
            pltpu.VMEM((2 * half, width), jnp.bfloat16),
            pltpu.VMEM((2 * half, owned * units), jnp.bfloat16),
        ],
        compiler_params=pltpu.CompilerParams(vmem_limit_bytes=VMEM_LIMIT),
        cost_estimate=cost(2 * half, weights[0]),
    )(b, a, shares, *weights)


def finish_kernel(*refs):
    terms, (out_ref, total_ref, sems) = refs[:-3], refs[-3:]
    half = terms[0].shape[0]
    copies = []
    for i in range(2):
        rows = pl.ds(i * half, half)
        total = sum(ref[...].astype(jnp.float32) for ref in terms[3 * i:3 * i + 3])
        total_ref[rows, :] = total.astype(total_ref.dtype)
        copies.append(pltpu.make_async_copy(total_ref.at[rows], out_ref.at[rows], sems.at[i]))
        copies[i].start()
    for copy in copies:
        copy.wait()


def finish(a, b):
    half, width = a[0].shape
    return pl.pallas_call(
        finish_kernel,
        in_specs=[pl.BlockSpec(memory_space=pltpu.VMEM)] * 6,
        out_specs=pl.BlockSpec(memory_space=pl.ANY),
        out_shape=jax.ShapeDtypeStruct((2 * half, width), a[0].dtype),
        scratch_shapes=[pltpu.VMEM((2 * half, width), a[0].dtype), pltpu.SemaphoreType.DMA((2,))],
        compiler_params=pltpu.CompilerParams(vmem_limit_bytes=VMEM_LIMIT),
    )(*a, *b)


def add(a, b):
    return (a.astype(jnp.float32) + b.astype(jnp.float32)).astype(jnp.bfloat16)


def body(tokens, target, router_weight, replica_pick, w_gate, w_up, w_down):
    height, width = tokens.shape
    half = height // 2
    groups = lax.axis_size("expert")
    slots = groups * (w_gate.shape[0] + 1)
    walk = ring_order(groups)
    ahead = [(walk[i], walk[(i + 1) % groups]) for i in range(groups)]
    back = [(b, a) for a, b in ahead]
    me = lax.axis_index("expert").astype(jnp.int32)
    after = jnp.where(me == groups - 1, 0, me + 1)
    place = jnp.stack([me, after, replica_pick[0]])
    weights = w_gate, w_up, w_down.reshape(-1, width)
    far = groups // 2

    a, b = tokens[:half], tokens[half:]
    lead_a, lead_b = pack(a, b, target, router_weight, slots)
    run = functools.partial(lead, place, weights, slots)
    own_a, own_b, shares = run(lead_a, lead_b)
    earlier = (shares,)
    parts = {}
    for s in range(1, far):
        lead_a = lax.ppermute(lead_a, "expert", ahead)
        lead_b = lax.ppermute(lead_b, "expert", back)
        b = lax.ppermute(b, "expert", ahead)
        a = lax.ppermute(a, "expert", back)
        lead_part_a, lead_part_b, shares = run(lead_a, lead_b, earlier)
        part_b, part_a, b, a = plain(weights, b, a, shares)
        earlier = ()
        parts[s] = lead_part_a, lead_part_b, part_b, part_a
    far_a, far_b, _ = run(lax.ppermute(lead_a, "expert", ahead), lax.ppermute(lead_b, "expert", back))

    lead_a, lead_b, a, b = lax.ppermute(far_a, "expert", back), lax.ppermute(far_b, "expert", ahead), None, None
    for s in range(far - 1, 0, -1):
        lead_part_a, lead_part_b, part_b, part_a = parts[s]
        b = lax.ppermute(part_b if b is None else add(part_b, b), "expert", back)
        a = lax.ppermute(part_a if a is None else add(part_a, a), "expert", ahead)
        lead_a = lax.ppermute(add(lead_part_a, lead_a), "expert", back)
        lead_b = lax.ppermute(add(lead_part_b, lead_b), "expert", ahead)
    return finish((own_a, lead_a, a), (own_b, lead_b, b))


def solution(mesh):
    in_specs = (
        P(("dp", "expert"), None),
        P(("dp", "expert"), None),
        P(("dp", "expert"), None),
        P(("dp", "expert")),
        P("expert", None, None),
        P("expert", None, None),
        P("expert", None, None),
    )
    out_specs = P(("dp", "expert"), None)
    return jax.shard_map(body, mesh=mesh, in_specs=in_specs, out_specs=out_specs, check_vma=False)
```

```python
import functools

import jax
import jax.numpy as jnp
import numpy as np
from jax import lax
from jax.experimental import pallas as pl
from jax.experimental.pallas import tpu as pltpu
from jax.sharding import PartitionSpec as P

VMEM_LIMIT = 12 * 1024 * 1024


def grid_of(groups):
    columns = 1 << ((groups.bit_length() - 1) // 2)
    return groups // columns, columns


def ring_order(groups):
    rows, columns = grid_of(groups)
    walk = [z * columns for z in range(rows)]
    for turn, z in enumerate(reversed(range(rows))):
        row = [z * columns + x for x in range(1, columns)]
        walk += row if turn % 2 == 0 else row[::-1]
    return walk


def table_rows(slots):
    return -(-slots // 16) * 16


def pack_kernel(slots, tokens_ref, target_ref, weight_ref, *outs):
    height, width = tokens_ref.shape
    half = height // 2
    across = width // half
    weight = weight_ref[...]
    share = weight / jnp.sum(weight, axis=0, keepdims=True)
    target = target_ref[...]
    row = lax.broadcasted_iota(jnp.int32, (table_rows(slots), height), 0)
    block = jnp.zeros(row.shape, jnp.float32)
    for slot in range(slots):
        value = jnp.sum(jnp.where(target == slot, share, 0.0), axis=0, keepdims=True)
        block = jnp.where(row == slot, value, block)
    for k, out_ref in enumerate(outs):
        for i in range(half // 16):
            for j in range(across):
                tile = tokens_ref[k * half + i * 16:k * half + i * 16 + 16, j * half:(j + 1) * half]
                out_ref[(i * across + j) * 16:(i * across + j) * 16 + 16, :] = tile
        out_ref[width:, :] = block[:, k * half:(k + 1) * half].astype(jnp.bfloat16)


def pack(tokens, target, router_weight, slots):
    height, width = tokens.shape
    half = height // 2
    vmem = pl.BlockSpec(memory_space=pltpu.VMEM)
    return pl.pallas_call(
        functools.partial(pack_kernel, slots),
        in_specs=[vmem] * 3,
        out_specs=[vmem] * 2,
        out_shape=[jax.ShapeDtypeStruct((width + table_rows(slots), half), jnp.bfloat16)] * 2,
        compiler_params=pltpu.CompilerParams(vmem_limit_bytes=VMEM_LIMIT),
        cost_estimate=pl.CostEstimate(flops=0, bytes_accessed=4 * height * width, transcendentals=0),
    )(tokens, target.T, router_weight.T)


def columns(place_ref, chunk_ref, slots, owned):
    rows, half = chunk_ref.shape
    me, after, pick = place_ref[0], place_ref[1], place_ref[2]
    block = chunk_ref[rows - table_rows(slots):, :].astype(jnp.float32)
    row = lax.broadcasted_iota(jnp.int32, block.shape, 0)

    def column(slot):
        return jnp.sum(jnp.where(row == slot, block, 0.0), axis=0, keepdims=True)

    lent = column(after * (owned + 1) + owned)
    line_of = lax.broadcasted_iota(jnp.int32, (128, half), 0)
    shares = jnp.zeros((128, half), jnp.float32)
    for e in range(owned):
        line = column(me * (owned + 1) + e) + jnp.where(pick == e, lent, 0.0)
        shares = jnp.where(line_of == e, line, shares)
    return shares.T


def evaluate(rows_ref, share_ref, gate_ref, up_ref, down_ref, outs, hidden_ref):
    half, width = outs[0].shape
    owned, _, units = gate_ref.shape
    wide = width // 2 if width % 256 == 0 else width

    def project(e, carry):
        x = rows_ref[...]
        gate = jnp.dot(x, gate_ref[e], preferred_element_type=jnp.float32)
        upper = jnp.dot(x, up_ref[e], preferred_element_type=jnp.float32)
        shares = share_ref[...]
        lane = lax.broadcasted_iota(jnp.int32, shares.shape, 1)
        share = jnp.sum(jnp.where(lane == e, shares, 0.0), axis=1, keepdims=True)
        hidden = gate / (1.0 + jnp.exp(-gate)) * upper * share
        hidden_ref[:, pl.ds(pl.multiple_of(e * units, units), units)] = hidden.astype(jnp.bfloat16)
        return carry

    lax.fori_loop(0, owned, project, 0)

    def fold(j, carry):
        at = pl.ds(pl.multiple_of(j * wide, wide), wide)
        part = jnp.dot(hidden_ref[...], down_ref[:, at], preferred_element_type=jnp.float32)
        for i, out_ref in enumerate(outs):
            out_ref[:, at] = part[i * half:(i + 1) * half].astype(jnp.bfloat16)
        return carry

    lax.fori_loop(0, width // wide, fold, 0)


def cost(rows, w_gate):
    owned, width, units = w_gate.shape
    return pl.CostEstimate(
        flops=6 * rows * width * units * owned, bytes_accessed=8 * rows * width, transcendentals=rows * units * owned
    )


def pair_kernel(slots, count, first, place_ref, *refs):
    chunks = refs[:count]
    gate_ref, up_ref, down_ref = refs[count:count + 3]
    outs = refs[count + 3:count + 5]
    picked_ref, rows_ref, share_ref, hidden_ref, sems = refs[count + 5:]
    owned = gate_ref.shape[0]
    half, width = outs[0].shape
    across = width // half
    for k in range(2):
        for i, chunk in enumerate(chunks):
            @pl.when(place_ref[first + k] == i)
            def _(k=k, chunk=chunk):
                pltpu.make_async_copy(chunk, picked_ref.at[k], sems.at[k]).start()
    for k in range(2):
        pltpu.make_async_copy(chunks[0], picked_ref.at[k], sems.at[k]).wait()
        for i in range(half // 16):
            for j in range(across):
                tile = picked_ref[k, (i * across + j) * 16:(i * across + j) * 16 + 16, :]
                rows_ref[k * half + i * 16:k * half + i * 16 + 16, j * half:(j + 1) * half] = tile
        share_ref[k * half:(k + 1) * half, :] = columns(place_ref, picked_ref.at[k], slots, owned)
    evaluate(rows_ref, share_ref, gate_ref, up_ref, down_ref, outs, hidden_ref)


def pair(place, weights, slots, chunks, first):
    (packed, half), (owned, width, units) = chunks[0].shape, weights[0].shape
    vmem, anywhere = pl.BlockSpec(memory_space=pltpu.VMEM), pl.BlockSpec(memory_space=pl.ANY)
    return pl.pallas_call(
        functools.partial(pair_kernel, slots, len(chunks), first),
        in_specs=[pl.BlockSpec(memory_space=pltpu.SMEM)] + [anywhere] * len(chunks) + [vmem] * 3,
        out_specs=[vmem] * 2,
        out_shape=[jax.ShapeDtypeStruct((half, width), jnp.bfloat16)] * 2,
        scratch_shapes=[
            pltpu.VMEM((2, packed, half), jnp.bfloat16),
            pltpu.VMEM((2 * half, width), jnp.bfloat16),
            pltpu.VMEM((2 * half, 128), jnp.float32),
            pltpu.VMEM((2 * half, owned * units), jnp.bfloat16),
            pltpu.SemaphoreType.DMA((2,)),
        ],
        compiler_params=pltpu.CompilerParams(vmem_limit_bytes=VMEM_LIMIT),
        cost_estimate=cost(2 * half, weights[0]),
    )(place, *chunks, *weights)


def finish_kernel(counts, *refs):
    terms, (out_ref, total_ref, sems) = refs[:-3], refs[-3:]
    half = terms[0].shape[0]
    copies = []
    for i, group in enumerate((terms[:counts[0]], terms[counts[0]:])):
        rows = pl.ds(i * half, half)
        total = sum(ref[...].astype(jnp.float32) for ref in group)
        total_ref[rows, :] = total.astype(total_ref.dtype)
        copies.append(pltpu.make_async_copy(total_ref.at[rows], out_ref.at[rows], sems.at[i]))
        copies[i].start()
    for copy in copies:
        copy.wait()


def finish(a, b):
    half, width = a[0].shape
    return pl.pallas_call(
        functools.partial(finish_kernel, (len(a), len(b))),
        in_specs=[pl.BlockSpec(memory_space=pltpu.VMEM)] * (len(a) + len(b)),
        out_specs=pl.BlockSpec(memory_space=pl.ANY),
        out_shape=jax.ShapeDtypeStruct((2 * half, width), a[0].dtype),
        scratch_shapes=[pltpu.VMEM((2 * half, width), a[0].dtype), pltpu.SemaphoreType.DMA((2,))],
        compiler_params=pltpu.CompilerParams(vmem_limit_bytes=VMEM_LIMIT),
    )(*a, *b)


def add(*terms):
    return sum(term.astype(jnp.float32) for term in terms).astype(jnp.bfloat16)


def ring_gather(own, groups, move, select, back_first):
    walk = ring_order(groups)
    ahead = [(walk[i], walk[(i + 1) % groups]) for i in range(groups)]
    back = [(j, i) for i, j in ahead]
    far = groups // 2
    chains = []
    for pairs, steps in ((ahead, far - back_first), (back, far - 1 + back_first)):
        chain = [own]
        for _ in range(steps):
            chain.append(move(chain[-1], pairs))
        chains.append(chain[1:])
    return [own] + chains[0] + chains[1]


def ring_scatter(parts, groups, move, back_first):
    walk = ring_order(groups)
    ahead = [(walk[i], walk[(i + 1) % groups]) for i in range(groups)]
    back = [(j, i) for i, j in ahead]
    far = groups // 2
    counts = far - back_first, far - 1 + back_first
    sums = [None, None]
    for step in range(far, 0, -1):
        for k, pairs in ((0, back), (1, ahead)):
            if step <= counts[k]:
                part = parts(step if k == 0 else counts[0] + step)
                sums[k] = move(part if sums[k] is None else add(part, sums[k]), pairs)
    return [parts(0)] + sums


def grid_pairs(groups):
    rows, columns = grid_of(groups)
    at = lambda z, x: z * columns + x
    swap = [(at(z, x), at(z, 1 - x)) for z in range(rows) for x in range(columns)]
    end = [(at(z, x), at(z ^ 1, x)) for z in range(rows) for x in range(columns)]
    middle = [(at(z, x), at(rows - 1 - z, x)) for z in (1, 2) for x in range(columns)]
    out = [(at(z, x), at(z ^ 1, x)) for z in (0, 3) for x in range(columns)]
    return swap, end, middle, out, [(j, i) for i, j in out]


def grid_gather(own, groups, move, select):
    swap, end, middle, _, inward = grid_pairs(groups)
    v1, v2, m4 = move(own, swap), move(own, end), move(own, middle)
    m6, m5, v3 = move(v2, middle), move(v1, middle), move(v2, swap)
    v6 = select(m6, move(m6, inward))
    v4 = select(m4, move(m4, inward))
    v5 = select(m5, move(m5, inward))
    v7 = move(v6, swap)
    return [own, v1, v2, v3, v4, v5, v6, v7]


def grid_scatter(parts, groups, move):
    swap, end, middle, outward, _ = grid_pairs(groups)
    s6 = add(parts(6), move(parts(7), swap))
    s6 = add(s6, move(s6, outward))
    s5 = add(parts(5), move(parts(5), outward))
    s4 = add(parts(4), move(parts(4), outward))
    s2 = add(parts(2), move(parts(3), swap), move(s6, middle))
    s1 = add(parts(1), move(s5, middle))
    return [parts(0), move(s4, middle), move(s2, end), move(s1, swap)]


def body(tokens, target, router_weight, replica_pick, w_gate, w_up, w_down):
    width = tokens.shape[1]
    groups = lax.axis_size("expert")
    slots = groups * (w_gate.shape[0] + 1)
    rows, columns_of = grid_of(groups)
    gridded = (rows, columns_of) == (4, 2)
    me = lax.axis_index("expert").astype(jnp.int32)
    inner = (me // columns_of) % (rows - 1) != 0

    def move(value, pairs):
        return lax.ppermute(value, "expert", pairs)

    def select(mine, other):
        return jnp.where(inner, mine, other)

    def move_index(value, pairs):
        result = np.zeros_like(value)
        for i, j in pairs:
            result[j] = value[i]
        return result

    is_inner = np.array([(i // columns_of) % (rows - 1) != 0 for i in range(groups)])
    ring = [functools.partial(ring_gather, back_first=k) for k in range(2)]
    gathers = [ring[0], grid_gather if gridded else ring[1]]
    scatter_maps = [grid_gather if gridded else ring[0], ring[0]]
    scatters = [grid_scatter if gridded else functools.partial(ring_scatter, back_first=0),
                functools.partial(ring_scatter, back_first=0)]
    far = groups // 2
    ring_calls = [(far - i, far + far - 1 - i) for i in range(far - 1)] + [(1, 0)]
    calls = [[(7, 6), (5, 4), (3, 2), (1, 0)] if gridded else ring_calls, ring_calls]

    entries = [np.arange(groups), (np.arange(groups) + 1) % groups, np.zeros(groups, int)]
    plans = []
    for k in range(2):
        owners = [f(np.arange(groups), groups, move_index, lambda a, b: np.where(is_inner, a, b))
                  for f in (gathers[k], scatter_maps[k])]
        plan = {}
        for call in calls[k]:
            held = [[next(i for i in range(groups) if owners[0][i][d] == owners[1][slot][d]) for d in range(groups)]
                    for slot in call]
            used = sorted(set(held[0] + held[1]))
            plan[call] = used, len(entries)
            entries += [np.array([used.index(i) for i in line]) for line in held]
        plans.append(plan)
    table = jnp.asarray(np.stack(entries, axis=1), jnp.int32)
    place = lax.dynamic_index_in_dim(table, me, 0, keepdims=False)
    place = lax.dynamic_update_slice(place, replica_pick, (2,))

    weights = w_gate, w_up, w_down.reshape(-1, width)
    totals = []
    for k, own in enumerate(pack(tokens, target, router_weight, slots)):
        chunks = gathers[k](own, groups, move, select)
        done = {}

        def parts(slot, k=k, chunks=chunks, done=done):
            if slot not in done:
                call = next(c for c in calls[k] if slot in c)
                used, first = plans[k][call]
                done.update(zip(call, pair(place, weights, slots, [chunks[i] for i in used], first)))
            return done[slot]

        totals.append(scatters[k](parts, groups, move))
    return finish(*totals)


def solution(mesh):
    in_specs = (
        P(("dp", "expert"), None),
        P(("dp", "expert"), None),
        P(("dp", "expert"), None),
        P(("dp", "expert")),
        P("expert", None, None),
        P("expert", None, None),
        P("expert", None, None),
    )
    out_specs = P(("dp", "expert"), None)
    return jax.shard_map(body, mesh=mesh, in_specs=in_specs, out_specs=out_specs, check_vma=False)
```

```python
import functools

import jax
import jax.numpy as jnp
from jax import lax
from jax.experimental import pallas as pl
from jax.experimental.pallas import tpu as pltpu
from jax.sharding import PartitionSpec as P

VMEM_LIMIT = 12 * 1024 * 1024


def ring_order(groups):
    columns = 1 << ((groups.bit_length() - 1) // 2)
    rows = groups // columns
    walk = [z * columns for z in range(rows)]
    for turn, z in enumerate(reversed(range(rows))):
        row = [z * columns + x for x in range(1, columns)]
        walk += row if turn % 2 == 0 else row[::-1]
    return walk


def table_rows(slots):
    return -(-2 * slots // 16) * 16


def tiles(half, width):
    across = width // half
    for i in range(half // 16):
        for j in range(across):
            at = (i * across + j) * 16
            yield slice(i * 16, i * 16 + 16), slice(j * half, (j + 1) * half), slice(at, at + 16)


def pack_kernel(slots, a_ref, b_ref, target_ref, weight_ref, out_a_ref, out_b_ref):
    half, width = a_ref.shape
    for rows, columns, packed in tiles(half, width):
        out_a_ref[packed, :] = a_ref[rows, columns]
        out_b_ref[packed, :] = b_ref[rows, columns]
    weight = weight_ref[...]
    share = weight / jnp.sum(weight, axis=0, keepdims=True)
    target = target_ref[...]
    row = lax.broadcasted_iota(jnp.int32, (table_rows(slots), half), 0)
    block = jnp.zeros(row.shape, jnp.float32)
    for slot in range(slots):
        value = jnp.sum(jnp.where(target == slot, share, 0.0), axis=0, keepdims=True)
        block = jnp.where(row == slot, value[:, :half], block)
        block = jnp.where(row == slots + slot, value[:, half:], block)
    out_a_ref[width:, :] = block.astype(jnp.bfloat16)
    out_b_ref[width:, :] = block.astype(jnp.bfloat16)


def pack(a, b, target, router_weight, slots):
    half, width = a.shape
    vmem = pl.BlockSpec(memory_space=pltpu.VMEM)
    return pl.pallas_call(
        functools.partial(pack_kernel, slots),
        in_specs=[vmem] * 4,
        out_specs=[vmem] * 2,
        out_shape=[jax.ShapeDtypeStruct((width + table_rows(slots), half), jnp.bfloat16)] * 2,
        compiler_params=pltpu.CompilerParams(vmem_limit_bytes=VMEM_LIMIT),
        cost_estimate=pl.CostEstimate(flops=0, bytes_accessed=8 * half * width, transcendentals=0),
    )(a, b, target.T, router_weight.T)


def columns(place_ref, lead_ref, index, slots, owned):
    rows, half = lead_ref.shape
    extra = table_rows(slots)
    me, after, pick = place_ref[0], place_ref[1], place_ref[2]
    block = lead_ref[rows - extra:, :].astype(jnp.float32)
    row = lax.broadcasted_iota(jnp.int32, block.shape, 0)

    def column(slot):
        return jnp.sum(jnp.where(row == index * slots + slot, block, 0.0), axis=0, keepdims=True)

    lent = column(after * (owned + 1) + owned)
    line_of = lax.broadcasted_iota(jnp.int32, (128, half), 0)
    shares = jnp.zeros((128, half), jnp.float32)
    for e in range(owned):
        line = column(me * (owned + 1) + e) + jnp.where(pick == e, lent, 0.0)
        shares = jnp.where(line_of == e, line, shares)
    return shares.T


def evaluate(rows_ref, share_ref, gate_ref, up_ref, down_ref, outs, hidden_ref):
    half, width = outs[0].shape
    owned, _, units = gate_ref.shape
    wide = width // 2 if width % 256 == 0 else width

    def project(e, carry):
        x = rows_ref[...]
        gate = jnp.dot(x, gate_ref[e], preferred_element_type=jnp.float32)
        upper = jnp.dot(x, up_ref[e], preferred_element_type=jnp.float32)
        shares = share_ref[...]
        lane = lax.broadcasted_iota(jnp.int32, shares.shape, 1)
        share = jnp.sum(jnp.where(lane == e, shares, 0.0), axis=1, keepdims=True)
        hidden = gate / (1.0 + jnp.exp(-gate)) * upper * share
        hidden_ref[:, pl.ds(pl.multiple_of(e * units, units), units)] = hidden.astype(jnp.bfloat16)
        return carry

    lax.fori_loop(0, owned, project, 0)

    def fold(j, carry):
        at = pl.ds(pl.multiple_of(j * wide, wide), wide)
        part = jnp.dot(hidden_ref[...], down_ref[:, at], preferred_element_type=jnp.float32)
        for i, out_ref in enumerate(outs):
            out_ref[:, at] = part[i * half:(i + 1) * half].astype(jnp.bfloat16)
        return carry

    lax.fori_loop(0, width // wide, fold, 0)


def lead_kernel(slots, place_ref, a_ref, b_ref, gate_ref, up_ref, down_ref, *refs):
    out_a_ref, out_b_ref, other_ref, rows_ref, share_ref, hidden_ref = refs[-6:]
    owned = gate_ref.shape[0]
    half, width = out_a_ref.shape
    for i, ref in enumerate((a_ref, b_ref)):
        at = slice(i * half, (i + 1) * half)
        for rows, across, packed in tiles(half, width):
            rows_ref[i * half + rows.start:i * half + rows.stop, across] = ref[packed, :]
        share_ref[at, :] = columns(place_ref, ref, i, slots, owned)
        other_ref[at, :] = columns(place_ref, ref, 1 - i, slots, owned)
    evaluate(rows_ref, share_ref, gate_ref, up_ref, down_ref, (out_a_ref, out_b_ref), hidden_ref)


def plain_kernel(b_ref, a_ref, share_ref, gate_ref, up_ref, down_ref, out_b_ref, out_a_ref, rows_ref, hidden_ref):
    half = b_ref.shape[0]
    rows_ref[:half, :] = b_ref[...]
    rows_ref[half:, :] = a_ref[...]
    evaluate(rows_ref, share_ref, gate_ref, up_ref, down_ref, (out_b_ref, out_a_ref), hidden_ref)


def cost(rows, w_gate):
    owned, width, units = w_gate.shape
    return pl.CostEstimate(
        flops=6 * rows * width * units * owned, bytes_accessed=8 * rows * width, transcendentals=rows * units * owned
    )


def lead(place, weights, slots, a, b, earlier=()):
    half, (owned, width, units) = a.shape[1], weights[0].shape
    height = 2 * half
    vmem = pl.BlockSpec(memory_space=pltpu.VMEM)
    return pl.pallas_call(
        functools.partial(lead_kernel, slots),
        in_specs=[pl.BlockSpec(memory_space=pltpu.SMEM)] + [vmem] * 5 + [pl.BlockSpec(memory_space=pl.ANY)] * len(earlier),
        out_specs=[vmem] * 3,
        out_shape=[jax.ShapeDtypeStruct((half, width), jnp.bfloat16)] * 2
        + [jax.ShapeDtypeStruct((height, 128), jnp.float32)],
        scratch_shapes=[
            pltpu.VMEM((height, width), jnp.bfloat16),
            pltpu.VMEM((height, 128), jnp.float32),
            pltpu.VMEM((height, owned * units), jnp.bfloat16),
        ],
        compiler_params=pltpu.CompilerParams(vmem_limit_bytes=VMEM_LIMIT),
        cost_estimate=cost(height, weights[0]),
    )(place, a, b, *weights, *earlier)


def plain(weights, b, a, shares):
    (half, width), (owned, _, units) = b.shape, weights[0].shape
    vmem = pl.BlockSpec(memory_space=pltpu.VMEM)
    return pl.pallas_call(
        plain_kernel,
        in_specs=[vmem] * 6,
        out_specs=[vmem] * 2,
        out_shape=[jax.ShapeDtypeStruct((half, width), jnp.bfloat16)] * 2,
        scratch_shapes=[
            pltpu.VMEM((2 * half, width), jnp.bfloat16),
            pltpu.VMEM((2 * half, owned * units), jnp.bfloat16),
        ],
        compiler_params=pltpu.CompilerParams(vmem_limit_bytes=VMEM_LIMIT),
        cost_estimate=cost(2 * half, weights[0]),
    )(b, a, shares, *weights)


def finish_kernel(*refs):
    terms, (out_ref, total_ref, sems) = refs[:-3], refs[-3:]
    half = terms[0].shape[0]
    copies = []
    for i in range(2):
        rows = pl.ds(i * half, half)
        total = sum(ref[...].astype(jnp.float32) for ref in terms[3 * i:3 * i + 3])
        total_ref[rows, :] = total.astype(total_ref.dtype)
        copies.append(pltpu.make_async_copy(total_ref.at[rows], out_ref.at[rows], sems.at[i]))
        copies[i].start()
    for copy in copies:
        copy.wait()


def finish(a, b):
    half, width = a[0].shape
    return pl.pallas_call(
        finish_kernel,
        in_specs=[pl.BlockSpec(memory_space=pltpu.VMEM)] * 6,
        out_specs=pl.BlockSpec(memory_space=pl.ANY),
        out_shape=jax.ShapeDtypeStruct((2 * half, width), a[0].dtype),
        scratch_shapes=[pltpu.VMEM((2 * half, width), a[0].dtype), pltpu.SemaphoreType.DMA((2,))],
        compiler_params=pltpu.CompilerParams(vmem_limit_bytes=VMEM_LIMIT),
    )(*a, *b)


def after_all(*values):
    return lax.optimization_barrier(values)


def add(a, b):
    return (a.astype(jnp.float32) + b.astype(jnp.float32)).astype(jnp.bfloat16)


def body(tokens, target, router_weight, replica_pick, w_gate, w_up, w_down):
    height, width = tokens.shape
    half = height // 2
    groups = lax.axis_size("expert")
    slots = groups * (w_gate.shape[0] + 1)
    walk = ring_order(groups)
    ahead = [(walk[i], walk[(i + 1) % groups]) for i in range(groups)]
    back = [(b, a) for a, b in ahead]
    me = lax.axis_index("expert").astype(jnp.int32)
    after = jnp.where(me == groups - 1, 0, me + 1)
    place = jnp.stack([me, after, replica_pick[0]])
    weights = w_gate, w_up, w_down.reshape(-1, width)
    far = groups // 2

    a, b = tokens[:half], tokens[half:]
    lead_a, lead_b = pack(a, b, target, router_weight, slots)
    run = functools.partial(lead, place, weights, slots)
    own_a, own_b, ended = run(lead_a, lead_b)
    parts = {}
    for s in range(1, far):
        b, a = lax.ppermute(b, "expert", ahead), lax.ppermute(a, "expert", back)
        lead_a, lead_b = lax.ppermute(lead_a, "expert", ahead), lax.ppermute(lead_b, "expert", back)
        lead_a, lead_b = after_all((lead_a, lead_b), ended)[0]
        lead_part_a, lead_part_b, shares = run(lead_a, lead_b, (ended,) if s == 1 else ())
        b, a = after_all((b, a), shares)[0]
        part_b, part_a = plain(weights, b, a, shares)
        ended = part_b
        parts[s] = lead_part_a, lead_part_b, part_b, part_a
    far_a, far_b, _ = run(lax.ppermute(lead_a, "expert", ahead), lax.ppermute(lead_b, "expert", back))

    lead_a, lead_b, a, b = lax.ppermute(far_a, "expert", back), lax.ppermute(far_b, "expert", ahead), None, None
    for s in range(far - 1, 0, -1):
        lead_part_a, lead_part_b, part_b, part_a = parts[s]
        b = lax.ppermute(part_b if b is None else add(part_b, b), "expert", back)
        a = lax.ppermute(part_a if a is None else add(part_a, a), "expert", ahead)
        lead_a = lax.ppermute(add(lead_part_a, lead_a), "expert", back)
        lead_b = lax.ppermute(add(lead_part_b, lead_b), "expert", ahead)
    return finish((own_a, lead_a, a), (own_b, lead_b, b))


def solution(mesh):
    in_specs = (
        P(("dp", "expert"), None),
        P(("dp", "expert"), None),
        P(("dp", "expert"), None),
        P(("dp", "expert")),
        P("expert", None, None),
        P("expert", None, None),
        P("expert", None, None),
    )
    out_specs = P(("dp", "expert"), None)
    return jax.shard_map(body, mesh=mesh, in_specs=in_specs, out_specs=out_specs, check_vma=False)
```

```python
import functools

import jax
import jax.numpy as jnp
from jax import lax
from jax.experimental import pallas as pl
from jax.experimental.pallas import tpu as pltpu
from jax.sharding import PartitionSpec as P

VMEM_LIMIT = 12 * 1024 * 1024


def ring_order(groups):
    columns = 1 << ((groups.bit_length() - 1) // 2)
    rows = groups // columns
    walk = [z * columns for z in range(rows)]
    for turn, z in enumerate(reversed(range(rows))):
        row = [z * columns + x for x in range(1, columns)]
        walk += row if turn % 2 == 0 else row[::-1]
    return walk


def table_rows(slots):
    return -(-2 * slots // 16) * 16


def tiles(half, width):
    across = width // half
    for i in range(half // 16):
        for j in range(across):
            at = (i * across + j) * 16
            yield slice(i * 16, i * 16 + 16), slice(j * half, (j + 1) * half), slice(at, at + 16)


def pack_kernel(slots, a_ref, b_ref, target_ref, weight_ref, out_a_ref, out_b_ref):
    half, width = a_ref.shape
    for rows, columns, packed in tiles(half, width):
        out_a_ref[packed, :] = a_ref[rows, columns]
        out_b_ref[packed, :] = b_ref[rows, columns]
    weight = weight_ref[...]
    share = weight / jnp.sum(weight, axis=0, keepdims=True)
    target = target_ref[...]
    row = lax.broadcasted_iota(jnp.int32, (table_rows(slots), half), 0)
    block = jnp.zeros(row.shape, jnp.float32)
    for slot in range(slots):
        value = jnp.sum(jnp.where(target == slot, share, 0.0), axis=0, keepdims=True)
        block = jnp.where(row == slot, value[:, :half], block)
        block = jnp.where(row == slots + slot, value[:, half:], block)
    out_a_ref[width:, :] = block.astype(jnp.bfloat16)
    out_b_ref[width:, :] = block.astype(jnp.bfloat16)


def pack(a, b, target, router_weight, slots):
    half, width = a.shape
    vmem = pl.BlockSpec(memory_space=pltpu.VMEM)
    return pl.pallas_call(
        functools.partial(pack_kernel, slots),
        in_specs=[vmem] * 4,
        out_specs=[vmem] * 2,
        out_shape=[jax.ShapeDtypeStruct((width + table_rows(slots), half), jnp.bfloat16)] * 2,
        compiler_params=pltpu.CompilerParams(vmem_limit_bytes=VMEM_LIMIT),
        cost_estimate=pl.CostEstimate(flops=0, bytes_accessed=8 * half * width, transcendentals=0),
    )(a, b, target.T, router_weight.T)


def columns(place_ref, lead_ref, index, slots, owned):
    rows, half = lead_ref.shape
    extra = table_rows(slots)
    me, after, pick = place_ref[0], place_ref[1], place_ref[2]
    block = lead_ref[rows - extra:, :].astype(jnp.float32)
    row = lax.broadcasted_iota(jnp.int32, block.shape, 0)

    def column(slot):
        return jnp.sum(jnp.where(row == index * slots + slot, block, 0.0), axis=0, keepdims=True)

    lent = column(after * (owned + 1) + owned)
    line_of = lax.broadcasted_iota(jnp.int32, (128, half), 0)
    shares = jnp.zeros((128, half), jnp.float32)
    for e in range(owned):
        line = column(me * (owned + 1) + e) + jnp.where(pick == e, lent, 0.0)
        shares = jnp.where(line_of == e, line, shares)
    return shares.T


def evaluate(rows_ref, share_ref, gate_ref, up_ref, down_ref, outs, hidden_ref):
    half, width = outs[0].shape
    owned, _, units = gate_ref.shape
    wide = width // 2 if width % 256 == 0 else width

    def project(e, carry):
        x = rows_ref[...]
        gate = jnp.dot(x, gate_ref[e], preferred_element_type=jnp.float32)
        upper = jnp.dot(x, up_ref[e], preferred_element_type=jnp.float32)
        shares = share_ref[...]
        lane = lax.broadcasted_iota(jnp.int32, shares.shape, 1)
        share = jnp.sum(jnp.where(lane == e, shares, 0.0), axis=1, keepdims=True)
        hidden = gate / (1.0 + jnp.exp(-gate)) * upper * share
        hidden_ref[:, pl.ds(pl.multiple_of(e * units, units), units)] = hidden.astype(jnp.bfloat16)
        return carry

    lax.fori_loop(0, owned, project, 0)

    def fold(j, carry):
        at = pl.ds(pl.multiple_of(j * wide, wide), wide)
        part = jnp.dot(hidden_ref[...], down_ref[:, at], preferred_element_type=jnp.float32)
        for i, out_ref in enumerate(outs):
            out_ref[:, at] = part[i * half:(i + 1) * half].astype(jnp.bfloat16)
        return carry

    lax.fori_loop(0, width // wide, fold, 0)


def lead_kernel(slots, place_ref, a_ref, b_ref, gate_ref, up_ref, down_ref, *refs):
    out_a_ref, out_b_ref, other_ref, rows_ref, share_ref, hidden_ref = refs[-6:]
    owned = gate_ref.shape[0]
    half, width = out_a_ref.shape
    for i, ref in enumerate((a_ref, b_ref)):
        at = slice(i * half, (i + 1) * half)
        for rows, across, packed in tiles(half, width):
            rows_ref[i * half + rows.start:i * half + rows.stop, across] = ref[packed, :]
        share_ref[at, :] = columns(place_ref, ref, i, slots, owned)
        other_ref[at, :] = columns(place_ref, ref, 1 - i, slots, owned)
    evaluate(rows_ref, share_ref, gate_ref, up_ref, down_ref, (out_a_ref, out_b_ref), hidden_ref)


def plain_kernel(b_ref, a_ref, share_ref, gate_ref, up_ref, down_ref, out_b_ref, out_a_ref, rows_ref, hidden_ref):
    half = b_ref.shape[0]
    rows_ref[:half, :] = b_ref[...]
    rows_ref[half:, :] = a_ref[...]
    evaluate(rows_ref, share_ref, gate_ref, up_ref, down_ref, (out_b_ref, out_a_ref), hidden_ref)


def cost(rows, w_gate):
    owned, width, units = w_gate.shape
    return pl.CostEstimate(
        flops=6 * rows * width * units * owned, bytes_accessed=8 * rows * width, transcendentals=rows * units * owned
    )


def lead(place, weights, slots, a, b, earlier=()):
    half, (owned, width, units) = a.shape[1], weights[0].shape
    height = 2 * half
    vmem = pl.BlockSpec(memory_space=pltpu.VMEM)
    return pl.pallas_call(
        functools.partial(lead_kernel, slots),
        in_specs=[pl.BlockSpec(memory_space=pltpu.SMEM)] + [vmem] * 5 + [pl.BlockSpec(memory_space=pl.ANY)] * len(earlier),
        out_specs=[vmem] * 3,
        out_shape=[jax.ShapeDtypeStruct((half, width), jnp.bfloat16)] * 2
        + [jax.ShapeDtypeStruct((height, 128), jnp.float32)],
        scratch_shapes=[
            pltpu.VMEM((height, width), jnp.bfloat16),
            pltpu.VMEM((height, 128), jnp.float32),
            pltpu.VMEM((height, owned * units), jnp.bfloat16),
        ],
        compiler_params=pltpu.CompilerParams(vmem_limit_bytes=VMEM_LIMIT),
        cost_estimate=cost(height, weights[0]),
    )(place, a, b, *weights, *earlier)


def plain(weights, b, a, shares):
    (half, width), (owned, _, units) = b.shape, weights[0].shape
    vmem = pl.BlockSpec(memory_space=pltpu.VMEM)
    return pl.pallas_call(
        plain_kernel,
        in_specs=[vmem] * 6,
        out_specs=[vmem] * 2,
        out_shape=[jax.ShapeDtypeStruct((half, width), jnp.bfloat16)] * 2,
        scratch_shapes=[
            pltpu.VMEM((2 * half, width), jnp.bfloat16),
            pltpu.VMEM((2 * half, owned * units), jnp.bfloat16),
        ],
        compiler_params=pltpu.CompilerParams(vmem_limit_bytes=VMEM_LIMIT),
        cost_estimate=cost(2 * half, weights[0]),
    )(b, a, shares, *weights)


def early_kernel(*refs):
    refs[-1][...] = sum(ref[...].astype(jnp.float32) for ref in refs[:-1])


def early(terms):
    vmem = pl.BlockSpec(memory_space=pltpu.VMEM)
    return pl.pallas_call(
        early_kernel,
        in_specs=[vmem] * len(terms),
        out_specs=vmem,
        out_shape=jax.ShapeDtypeStruct(terms[0].shape, jnp.float32),
        compiler_params=pltpu.CompilerParams(vmem_limit_bytes=VMEM_LIMIT),
    )(*terms)


def finish_kernel(*refs):
    terms, (out_ref, total_ref, sems) = refs[:-3], refs[-3:]
    half = terms[0].shape[0]
    quarter = half // 2
    copies = []
    for i in range(4):
        rows, part = pl.ds(i * quarter, quarter), pl.ds(i % 2 * quarter, quarter)
        total = sum(ref[part, :].astype(jnp.float32) for ref in terms[i // 2 * 2:i // 2 * 2 + 2])
        total_ref[rows, :] = total.astype(total_ref.dtype)
        copies.append(pltpu.make_async_copy(total_ref.at[rows], out_ref.at[rows], sems.at[i]))
        copies[i].start()
    for copy in copies:
        copy.wait()


def finish(a, b):
    half, width = a[0].shape
    return pl.pallas_call(
        finish_kernel,
        in_specs=[pl.BlockSpec(memory_space=pltpu.VMEM)] * 4,
        out_specs=pl.BlockSpec(memory_space=pl.ANY),
        out_shape=jax.ShapeDtypeStruct((2 * half, width), jnp.bfloat16),
        scratch_shapes=[pltpu.VMEM((2 * half, width), jnp.bfloat16), pltpu.SemaphoreType.DMA((4,))],
        compiler_params=pltpu.CompilerParams(vmem_limit_bytes=VMEM_LIMIT),
    )(*a, *b)


def after_all(*values):
    return lax.optimization_barrier(values)


def add(a, b):
    return (a.astype(jnp.float32) + b.astype(jnp.float32)).astype(jnp.bfloat16)


def body(tokens, target, router_weight, replica_pick, w_gate, w_up, w_down):
    height, width = tokens.shape
    half = height // 2
    groups = lax.axis_size("expert")
    slots = groups * (w_gate.shape[0] + 1)
    walk = ring_order(groups)
    ahead = [(walk[i], walk[(i + 1) % groups]) for i in range(groups)]
    back = [(b, a) for a, b in ahead]
    me = lax.axis_index("expert").astype(jnp.int32)
    after = jnp.where(me == groups - 1, 0, me + 1)
    place = jnp.stack([me, after, replica_pick[0]])
    weights = w_gate, w_up, w_down.reshape(-1, width)
    far = groups // 2

    a, b = tokens[:half], tokens[half:]
    lead_a, lead_b = pack(a, b, target, router_weight, slots)
    run = functools.partial(lead, place, weights, slots)
    own_a, own_b, ended = run(lead_a, lead_b)
    parts = {}
    for s in range(1, far):
        b, a = lax.ppermute(b, "expert", ahead), lax.ppermute(a, "expert", back)
        lead_a, lead_b = lax.ppermute(lead_a, "expert", ahead), lax.ppermute(lead_b, "expert", back)
        lead_a, lead_b = after_all((lead_a, lead_b), ended)[0]
        lead_part_a, lead_part_b, shares = run(lead_a, lead_b, (ended,) if s == 1 else ())
        b, a = after_all((b, a), shares)[0]
        part_b, part_a = plain(weights, b, a, shares)
        ended = part_b
        parts[s] = lead_part_a, lead_part_b, part_b, part_a
    far_a, far_b, _ = run(lax.ppermute(lead_a, "expert", ahead), lax.ppermute(lead_b, "expert", back))

    lead_a, lead_b, a, b = lax.ppermute(far_a, "expert", back), lax.ppermute(far_b, "expert", ahead), None, None
    for s in range(far - 1, 0, -1):
        lead_part_a, lead_part_b, part_b, part_a = parts[s]
        lead_b = lax.ppermute(add(lead_part_b, lead_b), "expert", ahead)
        lead_a = lax.ppermute(add(lead_part_a, lead_a), "expert", back)
        a = lax.ppermute(part_a if a is None else add(part_a, a), "expert", ahead)
        b = lax.ppermute(part_b if b is None else add(part_b, b), "expert", back)
    return finish((early((own_a, a)), lead_a), (early((own_b, b)), lead_b))


def solution(mesh):
    in_specs = (
        P(("dp", "expert"), None),
        P(("dp", "expert"), None),
        P(("dp", "expert"), None),
        P(("dp", "expert")),
        P("expert", None, None),
        P("expert", None, None),
        P("expert", None, None),
    )
    out_specs = P(("dp", "expert"), None)
    return jax.shard_map(body, mesh=mesh, in_specs=in_specs, out_specs=out_specs, check_vma=False)
```

```python
import functools

import jax
import jax.numpy as jnp
from jax import lax
from jax.experimental import pallas as pl
from jax.experimental.pallas import tpu as pltpu
from jax.sharding import PartitionSpec as P

VMEM_LIMIT = 12 * 1024 * 1024


def ring_order(groups):
    columns = 1 << ((groups.bit_length() - 1) // 2)
    rows = groups // columns
    walk = [z * columns for z in range(rows)]
    for turn, z in enumerate(reversed(range(rows))):
        row = [z * columns + x for x in range(1, columns)]
        walk += row if turn % 2 == 0 else row[::-1]
    return walk


def table_rows(top):
    return -(-4 * top // 16) * 16


def tiles(half, width):
    across = width // half
    for i in range(half // 16):
        for j in range(across):
            at = (i * across + j) * 16
            yield slice(i * 16, i * 16 + 16), slice(j * half, (j + 1) * half), slice(at, at + 16)


def pack_kernel(a_ref, b_ref, target_ref, weight_ref, out_a_ref, out_b_ref):
    half, width = a_ref.shape
    for rows, columns, packed in tiles(half, width):
        out_a_ref[packed, :] = a_ref[rows, columns]
        out_b_ref[packed, :] = b_ref[rows, columns]
    weight = weight_ref[...]
    share = weight / jnp.sum(weight, axis=0, keepdims=True)
    target = target_ref[...]
    top = target.shape[0]
    slot = target.astype(jnp.float32)
    lines = [part[:, i * half:(i + 1) * half] for i in range(2) for part in (slot, share)]
    spare = table_rows(top) - 4 * top
    if spare:
        lines.append(jnp.zeros((spare, half), jnp.float32))
    block = jnp.concatenate(lines, axis=0).astype(jnp.bfloat16)
    out_a_ref[width:, :] = block
    out_b_ref[width:, :] = block


def pack(a, b, target, router_weight):
    half, width = a.shape
    vmem = pl.BlockSpec(memory_space=pltpu.VMEM)
    return pl.pallas_call(
        pack_kernel,
        in_specs=[vmem] * 4,
        out_specs=[vmem] * 2,
        out_shape=[jax.ShapeDtypeStruct((width + table_rows(target.shape[1]), half), jnp.bfloat16)] * 2,
        compiler_params=pltpu.CompilerParams(vmem_limit_bytes=VMEM_LIMIT),
        cost_estimate=pl.CostEstimate(flops=0, bytes_accessed=8 * half * width, transcendentals=0),
    )(a, b, target.T, router_weight.T)


def columns(place_ref, lead_ref, index, top, owned):
    rows, half = lead_ref.shape
    me, after, pick = place_ref[0], place_ref[1], place_ref[2]
    block = lead_ref[rows - table_rows(top):, :].astype(jnp.float32)
    named = block[2 * index * top:(2 * index + 1) * top, :]
    share = block[(2 * index + 1) * top:(2 * index + 2) * top, :]

    def column(slot):
        return jnp.sum(jnp.where(named == slot.astype(jnp.float32), share, 0.0), axis=0, keepdims=True)

    lent = column(after * (owned + 1) + owned)
    line_of = lax.broadcasted_iota(jnp.int32, (128, half), 0)
    shares = jnp.zeros((128, half), jnp.float32)
    for e in range(owned):
        line = column(me * (owned + 1) + e) + jnp.where(pick == e, lent, 0.0)
        shares = jnp.where(line_of == e, line, shares)
    return shares.T


def evaluate(rows_ref, share_ref, gate_ref, up_ref, down_ref, outs, hidden_ref):
    half, width = outs[0].shape
    owned, _, units = gate_ref.shape
    wide = width // 2 if width % 256 == 0 else width

    def project(e, carry):
        x = rows_ref[...]
        gate = jnp.dot(x, gate_ref[e], preferred_element_type=jnp.float32)
        upper = jnp.dot(x, up_ref[e], preferred_element_type=jnp.float32)
        shares = share_ref[...]
        lane = lax.broadcasted_iota(jnp.int32, shares.shape, 1)
        share = jnp.sum(jnp.where(lane == e, shares, 0.0), axis=1, keepdims=True)
        hidden = gate / (1.0 + jnp.exp(-gate)) * upper * share
        hidden_ref[:, pl.ds(pl.multiple_of(e * units, units), units)] = hidden.astype(jnp.bfloat16)
        return carry

    lax.fori_loop(0, owned, project, 0)

    def fold(j, carry):
        at = pl.ds(pl.multiple_of(j * wide, wide), wide)
        part = jnp.dot(hidden_ref[...], down_ref[:, at], preferred_element_type=jnp.float32)
        for i, out_ref in enumerate(outs):
            out_ref[:, at] = part[i * half:(i + 1) * half].astype(jnp.bfloat16)
        return carry

    lax.fori_loop(0, width // wide, fold, 0)


def lead_kernel(top, place_ref, a_ref, b_ref, gate_ref, up_ref, down_ref, *refs):
    out_a_ref, out_b_ref, other_ref, rows_ref, share_ref, hidden_ref = refs[-6:]
    owned = gate_ref.shape[0]
    half, width = out_a_ref.shape
    for i, ref in enumerate((a_ref, b_ref)):
        at = slice(i * half, (i + 1) * half)
        for rows, across, packed in tiles(half, width):
            rows_ref[i * half + rows.start:i * half + rows.stop, across] = ref[packed, :]
        share_ref[at, :] = columns(place_ref, ref, i, top, owned)
        other_ref[at, :] = columns(place_ref, ref, 1 - i, top, owned)
    evaluate(rows_ref, share_ref, gate_ref, up_ref, down_ref, (out_a_ref, out_b_ref), hidden_ref)


def plain_kernel(b_ref, a_ref, share_ref, gate_ref, up_ref, down_ref, out_b_ref, out_a_ref, rows_ref, hidden_ref):
    half = b_ref.shape[0]
    rows_ref[:half, :] = b_ref[...]
    rows_ref[half:, :] = a_ref[...]
    evaluate(rows_ref, share_ref, gate_ref, up_ref, down_ref, (out_b_ref, out_a_ref), hidden_ref)


def cost(rows, w_gate):
    owned, width, units = w_gate.shape
    return pl.CostEstimate(
        flops=6 * rows * width * units * owned, bytes_accessed=8 * rows * width, transcendentals=rows * units * owned
    )


def lead(place, weights, top, a, b, earlier=()):
    half, (owned, width, units) = a.shape[1], weights[0].shape
    height = 2 * half
    vmem = pl.BlockSpec(memory_space=pltpu.VMEM)
    return pl.pallas_call(
        functools.partial(lead_kernel, top),
        in_specs=[pl.BlockSpec(memory_space=pltpu.SMEM)] + [vmem] * 5 + [pl.BlockSpec(memory_space=pl.ANY)] * len(earlier),
        out_specs=[vmem] * 3,
        out_shape=[jax.ShapeDtypeStruct((half, width), jnp.bfloat16)] * 2
        + [jax.ShapeDtypeStruct((height, 128), jnp.float32)],
        scratch_shapes=[
            pltpu.VMEM((height, width), jnp.bfloat16),
            pltpu.VMEM((height, 128), jnp.float32),
            pltpu.VMEM((height, owned * units), jnp.bfloat16),
        ],
        compiler_params=pltpu.CompilerParams(vmem_limit_bytes=VMEM_LIMIT),
        cost_estimate=cost(height, weights[0]),
    )(place, a, b, *weights, *earlier)


def plain(weights, b, a, shares):
    (half, width), (owned, _, units) = b.shape, weights[0].shape
    vmem = pl.BlockSpec(memory_space=pltpu.VMEM)
    return pl.pallas_call(
        plain_kernel,
        in_specs=[vmem] * 6,
        out_specs=[vmem] * 2,
        out_shape=[jax.ShapeDtypeStruct((half, width), jnp.bfloat16)] * 2,
        scratch_shapes=[
            pltpu.VMEM((2 * half, width), jnp.bfloat16),
            pltpu.VMEM((2 * half, owned * units), jnp.bfloat16),
        ],
        compiler_params=pltpu.CompilerParams(vmem_limit_bytes=VMEM_LIMIT),
        cost_estimate=cost(2 * half, weights[0]),
    )(b, a, shares, *weights)


def early_kernel(*refs):
    refs[-1][...] = sum(ref[...].astype(jnp.float32) for ref in refs[:-1])


def early(terms):
    vmem = pl.BlockSpec(memory_space=pltpu.VMEM)
    return pl.pallas_call(
        early_kernel,
        in_specs=[vmem] * len(terms),
        out_specs=vmem,
        out_shape=jax.ShapeDtypeStruct(terms[0].shape, jnp.float32),
        compiler_params=pltpu.CompilerParams(vmem_limit_bytes=VMEM_LIMIT),
    )(*terms)


def finish_kernel(*refs):
    terms, (out_ref, total_ref, sems) = refs[:-3], refs[-3:]
    half = terms[0].shape[0]
    quarter = half // 2
    copies = []
    for i in range(4):
        rows, part = pl.ds(i * quarter, quarter), pl.ds(i % 2 * quarter, quarter)
        total = sum(ref[part, :].astype(jnp.float32) for ref in terms[i // 2 * 2:i // 2 * 2 + 2])
        total_ref[rows, :] = total.astype(total_ref.dtype)
        copies.append(pltpu.make_async_copy(total_ref.at[rows], out_ref.at[rows], sems.at[i]))
        copies[i].start()
    for copy in copies:
        copy.wait()


def finish(a, b):
    half, width = a[0].shape
    return pl.pallas_call(
        finish_kernel,
        in_specs=[pl.BlockSpec(memory_space=pltpu.VMEM)] * 4,
        out_specs=pl.BlockSpec(memory_space=pl.ANY),
        out_shape=jax.ShapeDtypeStruct((2 * half, width), jnp.bfloat16),
        scratch_shapes=[pltpu.VMEM((2 * half, width), jnp.bfloat16), pltpu.SemaphoreType.DMA((4,))],
        compiler_params=pltpu.CompilerParams(vmem_limit_bytes=VMEM_LIMIT),
    )(*a, *b)


def after_all(*values):
    return lax.optimization_barrier(values)


def add(a, b):
    return (a.astype(jnp.float32) + b.astype(jnp.float32)).astype(jnp.bfloat16)


def body(tokens, target, router_weight, replica_pick, w_gate, w_up, w_down):
    height, width = tokens.shape
    half = height // 2
    groups = lax.axis_size("expert")
    walk = ring_order(groups)
    ahead = [(walk[i], walk[(i + 1) % groups]) for i in range(groups)]
    back = [(b, a) for a, b in ahead]
    me = lax.axis_index("expert").astype(jnp.int32)
    after = jnp.where(me == groups - 1, 0, me + 1)
    place = jnp.stack([me, after, replica_pick[0]])
    weights = w_gate, w_up, w_down.reshape(-1, width)
    far = groups // 2

    a, b = tokens[:half], tokens[half:]
    lead_a, lead_b = pack(a, b, target, router_weight)
    run = functools.partial(lead, place, weights, target.shape[1])
    own_a, own_b, ended = run(lead_a, lead_b)
    parts = {}
    for s in range(1, far):
        b, a = lax.ppermute(b, "expert", ahead), lax.ppermute(a, "expert", back)
        lead_a, lead_b = lax.ppermute(lead_a, "expert", ahead), lax.ppermute(lead_b, "expert", back)
        lead_a, lead_b = after_all((lead_a, lead_b), ended)[0]
        lead_part_a, lead_part_b, shares = run(lead_a, lead_b, (ended,) if s == 1 else ())
        b, a = after_all((b, a), shares)[0]
        part_b, part_a = plain(weights, b, a, shares)
        ended = part_b
        parts[s] = lead_part_a, lead_part_b, part_b, part_a
    far_a, far_b, _ = run(lax.ppermute(lead_a, "expert", ahead), lax.ppermute(lead_b, "expert", back))

    lead_a, lead_b, a, b = lax.ppermute(far_a, "expert", back), lax.ppermute(far_b, "expert", ahead), None, None
    for s in range(far - 1, 0, -1):
        lead_part_a, lead_part_b, part_b, part_a = parts[s]
        lead_b = lax.ppermute(add(lead_part_b, lead_b), "expert", ahead)
        lead_a = lax.ppermute(add(lead_part_a, lead_a), "expert", back)
        a = lax.ppermute(part_a if a is None else add(part_a, a), "expert", ahead)
        b = lax.ppermute(part_b if b is None else add(part_b, b), "expert", back)
    return finish((early((own_a, a)), lead_a), (early((own_b, b)), lead_b))


def solution(mesh):
    in_specs = (
        P(("dp", "expert"), None),
        P(("dp", "expert"), None),
        P(("dp", "expert"), None),
        P(("dp", "expert")),
        P("expert", None, None),
        P("expert", None, None),
        P("expert", None, None),
    )
    out_specs = P(("dp", "expert"), None)
    return jax.shard_map(body, mesh=mesh, in_specs=in_specs, out_specs=out_specs, check_vma=False)
```
